128 devices in a mesh: gz: 8 (over x, core), xy: 16 (over y, z).
Axes of the slice: x: 4, y: 4, z: 4, core: 2. Of those that a mesh axis runs over, the one named last changes fastest.
Arguments:
- patches: bfloat16 [2048, 128, 256], P(('gz', 'xy'))
- pair_leaves: int32 [24576, 2], P(('gz', 'xy')), may hold values from 0 to 2047, as said below
- pair_count: int32 [128], replicated, may hold values from 1 to 192, as said below
Outputs:
- denoised: bfloat16 [2048, 128, 256], P(('gz', 'xy'))
The draws below stay inside these ranges and needn't reach their ends.
Inputs may be any that keep to these rules, and one draw needn't show every extreme that they name: `pair_leaves`: row r belongs to device r // 192. Column 0 is a leaf held by that device; column 1 is a larger leaf id held by that device or one of the next two. Rows at or past that device's pair_count are ignored. `pair_count`: some device has exactly 192 live pairs.
All inputs are finite; a program needn't handle non-finite values.
Results may differ from the reference program's by a relative error of at most 0.005.
Values may be sent and summed in bfloat16 or wider, within the bound.
A program may use at most 64 MiB of HBM per device.

```python
import jax
import jax.numpy as jnp
from jax import lax

L_DEV = 16
LEAF = 128
PATCH = 256
PAIRS_DEV = 192
MOTIFS = 64
ROUNDS = 2
LEAVES = 2048


def draw_patches(key, part):
    key = jax.random.fold_in(key, 11)
    motif_key, pick_key, noise_key = jax.random.split(key, 3)
    motifs = jax.random.normal(motif_key, (MOTIFS, PATCH), jnp.float32)
    picks = jax.random.randint(pick_key, (LEAVES, LEAF), 0, MOTIFS)
    noise = 0.35 * jax.random.normal(noise_key, (LEAVES, LEAF, PATCH), jnp.float32)
    return (motifs[picks] + noise).astype(jnp.bfloat16)


def draw_pair_leaves(key, part):
    key = jax.random.fold_in(key, 12)
    local_key, reach_key = jax.random.split(key)
    devices = LEAVES // L_DEV
    rows = devices * PAIRS_DEV
    owner = jnp.arange(rows, dtype=jnp.int32) // PAIRS_DEV
    upper = jnp.where(owner == devices - 1, L_DEV - 1, L_DEV)
    local = jax.random.randint(local_key, (rows,), 0, upper)
    reach = jax.random.randint(reach_key, (rows,), 0, 3 * L_DEV - 1 - local)
    first = owner * L_DEV + local
    second = jnp.minimum(first + 1 + reach, LEAVES - 1)
    return jnp.stack([first, second], axis=1).astype(jnp.int32)


def draw_pair_count(key, part):
    key = jax.random.fold_in(key, 13)
    drawn_key, busy_key, heavy_key, chosen_key = jax.random.split(key, 4)
    devices = LEAVES // L_DEV
    drawn = jax.random.randint(drawn_key, (devices,), PAIRS_DEV * 3 // 10, PAIRS_DEV * 6 // 10 + 1)
    busy = jax.random.randint(busy_key, (devices,), PAIRS_DEV * 8 // 10, PAIRS_DEV + 1)
    heavy = jax.random.randint(heavy_key, (devices,), 0, 8) == 0
    chosen = jax.random.randint(chosen_key, (), 0, devices)
    counts = jnp.where(heavy, busy, drawn)
    counts = jnp.where(jnp.arange(devices) == chosen, PAIRS_DEV, counts)
    return counts.astype(jnp.int32)


def setup_inputs(seed: int = 0) -> dict:
    arg_keys = jax.random.split(jax.random.key(seed), 4)
    return {
        "patches": draw_patches(jax.random.fold_in(arg_keys[3], 71), 0),
        "pair_leaves": draw_pair_leaves(jax.random.fold_in(arg_keys[3], 71), 0),
        "pair_count": draw_pair_count(jax.random.fold_in(arg_keys[3], 71), 0),
    }


def denoise_round(current, pair_leaves, pair_count):
    width = current.shape[2]
    spread = width / 4.0
    rows = pair_leaves.shape[0]
    per_device = rows // pair_count.shape[0]
    flat = current.astype(jnp.float32)
    power = jnp.sum(flat * flat, axis=2)
    row_ids = jnp.arange(rows, dtype=jnp.int32)
    alive = (row_ids % per_device < pair_count[row_ids // per_device]).astype(jnp.float32)

    def advance(carry, item):
        numer, denom = carry
        record, living = item
        left_patch = flat[record[0]]
        right_patch = flat[record[1]]
        crossed = jnp.dot(left_patch, right_patch.T, preferred_element_type=jnp.float32, precision=lax.Precision.HIGHEST)
        distance = power[record[0]][:, None] + power[record[1]][None, :] - 2.0 * crossed
        weights = jnp.exp(-distance / spread) * living
        rounded = lax.optimization_barrier(weights.astype(jnp.bfloat16)).astype(jnp.float32)
        to_left = jnp.dot(rounded, right_patch, preferred_element_type=jnp.float32, precision=lax.Precision.HIGHEST)
        to_right = jnp.dot(rounded.T, left_patch, preferred_element_type=jnp.float32, precision=lax.Precision.HIGHEST)
        numer = numer.at[record[0]].add(to_left).at[record[1]].add(to_right)
        denom = denom.at[record[0]].add(jnp.sum(weights, axis=1)).at[record[1]].add(jnp.sum(weights, axis=0))
        return (numer, denom), None

    start = (jnp.zeros(flat.shape, jnp.float32), jnp.zeros(power.shape, jnp.float32))
    (numer, denom), _ = lax.scan(advance, start, (pair_leaves, alive))
    return ((flat + numer) / (1.0 + denom)[:, :, None]).astype(jnp.bfloat16)


def reference(patches, pair_leaves, pair_count):
    current = patches
    for round_index in range(ROUNDS):
        current = denoise_round(current, pair_leaves, pair_count)
    return current
```

```python
import functools
import math

import jax
import jax.numpy as jnp
from jax import lax
from jax.experimental import pallas as pl
from jax.experimental.pallas import tpu as pltpu
from jax.sharding import PartitionSpec as P

MESH = pl.DeviceIdType.MESH
ROUNDS = 2
OWN, NEXT, PREV, NEXT2, PREV2 = range(5)
CHUNKS = 8
GROUP = 4


def split(square):
    high = square.astype(jnp.bfloat16)
    low = (square - high.astype(jnp.float32)).astype(jnp.bfloat16)
    return high, low


def squares(block):
    wide = block.astype(jnp.float32)
    return split(wide * wide)


def contract(a, b, da, db):
    return lax.dot_general(
        a, b, (((da,), (db,)), ((), ())), preferred_element_type=jnp.float32
    )


def kernel(
    shape,
    sizes,
    count_ref,
    pairs_ref,
    patches_ref,
    out_ref,
    window,
    numer,
    denom,
    target_power,
    source_row,
    extra,
    listed,
    block_send,
    block_recv,
    listed_send,
    listed_recv,
):
    outer, inner = shape
    leaves, points = sizes
    devices = outer * inner
    rows = leaves * points
    chunk = rows // CHUNKS
    width = GROUP * points
    groups = leaves // GROUP
    per_group = CHUNKS // groups
    spread = patches_ref.shape[1] / 4.0
    scale = math.log2(math.e) / spread
    me = lax.axis_index("gz") * inner + lax.axis_index("xy")

    def device(step):
        index = lax.rem(me + step + devices, devices)
        return (index // inner, lax.rem(index, inner))

    barrier = pltpu.get_barrier_semaphore()
    for step in (1, -1, 2, -2):
        pl.semaphore_signal(barrier, inc=1, device_id=device(step), device_id_type=MESH)

    def block_copy(turn, slot, piece, step):
        place = pl.ds(pl.multiple_of(piece * chunk, chunk), chunk)
        source = {1: OWN, -1: OWN, 2: PREV, -2: NEXT}[step]
        toward = 1 if step > 0 else -1
        return pltpu.make_async_remote_copy(
            src_ref=window.at[turn, source, place],
            dst_ref=window.at[turn, slot, place],
            send_sem=block_send.at[turn, slot, piece],
            recv_sem=block_recv.at[turn, slot, piece],
            device_id=device(toward),
            device_id_type=MESH,
        )

    def to_next(turn, piece):
        return block_copy(turn, PREV, piece, 1)

    def to_prev(turn, piece):
        return block_copy(turn, NEXT, piece, -1)

    def on_to_next(turn, piece):
        return block_copy(turn, PREV2, piece, 2)

    def on_to_prev(turn, piece):
        return block_copy(turn, NEXT2, piece, -2)

    window[0, OWN] = patches_ref[...]
    pl.semaphore_wait(barrier, 4)

    def send_own(turn):
        def body(piece, _):
            to_next(turn, piece).start()
            to_prev(turn, piece).start()
            return 0

        lax.fori_loop(0, CHUNKS, body, 0)

    send_own(0)

    slots = pairs_ref.shape[0]
    lanes = 128
    lane = lax.broadcasted_iota(jnp.int32, (slots, lanes), 1)
    live = lax.broadcasted_iota(jnp.int32, (slots, lanes), 0) < count_ref[me]
    first = jnp.where(live & (pairs_ref[:, 0:1] - me * leaves == lane), 1.0, 0.0)
    second = jnp.where(live & (pairs_ref[:, 1:2] - me * leaves == lane), 1.0, 0.0)
    first, second = first.astype(jnp.bfloat16), second.astype(jnp.bfloat16)
    forward = contract(first, second, 0, 0)
    backward = contract(second, first, 0, 0)
    listed[0] = backward[leaves : 2 * leaves]
    listed[1] = backward[2 * leaves : 3 * leaves]

    def listed_copy(k):
        return pltpu.make_async_remote_copy(
            src_ref=listed.at[k],
            dst_ref=listed.at[2 + k],
            send_sem=listed_send.at[k],
            recv_sem=listed_recv.at[k],
            device_id=device(k + 1),
            device_id_type=MESH,
        )

    for k in range(2):
        listed_copy(k).start()

    def expand(counts, base):
        place = lax.broadcasted_iota(jnp.int32, (lanes, rows), 0) - base
        owner = lax.broadcasted_iota(jnp.int32, (lanes, rows), 1) // points
        spots = jnp.where(place == owner, 1.0, 0.0).astype(jnp.bfloat16)
        wide = contract(counts.astype(jnp.bfloat16), spots, 1, 0)
        return jnp.where(wide > 0.0, jnp.log2(wide), -jnp.inf)

    ahead = forward[:leaves]
    extra[OWN] = expand(ahead + backward[:leaves], 0)
    extra[NEXT] = expand(ahead, leaves)
    extra[NEXT2] = expand(ahead, 2 * leaves)
    for k in range(2):
        listed_copy(k).wait()
    extra[PREV] = expand(listed[2], 0)
    extra[PREV2] = expand(listed[3], 0)

    def unit(turn, slot, group):
        place = pl.ds(pl.multiple_of(group * width, width), width)
        source = window[turn, slot, place, :]
        high, low = squares(source)
        ones = jnp.ones((8, source.shape[1]), jnp.bfloat16)
        power = contract(ones, high, 1, 1) + contract(ones, low, 1, 1)
        source_row[...] = power[0:1] * scale - extra[slot, :, place]
        cross = contract(window[turn, OWN], source, 1, 1)
        parts = []
        for t in range(leaves):
            span = slice(t * points, (t + 1) * points)
            total, part = None, []
            for s in range(GROUP):
                lanes_here = slice(s * points, (s + 1) * points)
                away = target_power[span, :] + source_row[t : t + 1, lanes_here]
                weight = jnp.exp2(cross[span, lanes_here] * (2.0 * scale) - away)
                total = weight if total is None else total + weight
                part.append(weight.astype(jnp.bfloat16))
            denom[span, :] += total
            parts.append(jnp.concatenate(part, axis=1))
        weights = jnp.concatenate(parts, axis=0)
        numer[...] += jnp.dot(weights, source, preferred_element_type=jnp.float32)

    def one_round(turn, _):
        high, low = squares(window[turn, OWN])
        ones = jnp.ones((high.shape[1], points), jnp.bfloat16)
        target_power[...] = scale * (contract(high, ones, 1, 0) + contract(low, ones, 1, 0))
        numer[...] = jnp.zeros_like(numer)
        denom[...] = jnp.zeros_like(denom)

        def near(group, _):
            def arrive(k, _):
                piece = group * per_group + k
                to_next(turn, piece).wait_recv()
                on_to_next(turn, piece).start()
                to_prev(turn, piece).wait_recv()
                on_to_prev(turn, piece).start()
                return 0

            unit(turn, OWN, group)
            lax.fori_loop(0, per_group, arrive, 0)

            def each(k, _):
                unit(turn, NEXT + k, group)
                return 0

            lax.fori_loop(0, 2, each, 0)
            return 0

        def far(group, _):
            def arrive(k, _):
                piece = group * per_group + k
                on_to_next(turn, piece).wait_recv()
                on_to_prev(turn, piece).wait_recv()
                return 0

            lax.fori_loop(0, per_group, arrive, 0)

            def each(k, _):
                unit(turn, NEXT2 + k, group)
                return 0

            lax.fori_loop(0, 2, each, 0)
            return 0

        lax.fori_loop(0, groups, near, 0)
        lax.fori_loop(0, groups, far, 0)

        def finish(piece, _):
            place = pl.ds(pl.multiple_of(piece * chunk, chunk), chunk)
            below = 1.0 + jnp.sum(denom[place, :], axis=1, keepdims=True)
            above = window[turn, OWN, place, :].astype(jnp.float32) + numer[place, :]
            out_ref[place, :] = (above * (1.0 / below)).astype(jnp.bfloat16)

            @pl.when(turn + 1 < ROUNDS)
            def _():
                window[1, OWN, place, :] = out_ref[place, :]
                to_next(1, piece).start()
                to_prev(1, piece).start()

            return 0

        lax.fori_loop(0, CHUNKS, finish, 0)
        return 0

    lax.fori_loop(0, ROUNDS, one_round, 0)

    def drain(piece, _):
        for turn in range(ROUNDS):
            for copy in (to_next, to_prev, on_to_next, on_to_prev):
                copy(turn, piece).wait_send()
        return 0

    lax.fori_loop(0, CHUNKS, drain, 0)


def solution(mesh):
    shape = (mesh.shape["gz"], mesh.shape["xy"])

    def on_device(patches, pair_leaves, pair_count):
        leaves, points, values = patches.shape
        rows = leaves * points
        vmem = pl.BlockSpec(memory_space=pltpu.VMEM)
        out = pl.pallas_call(
            functools.partial(kernel, shape, (leaves, points)),
            out_shape=jax.ShapeDtypeStruct((rows, values), jnp.bfloat16),
            in_specs=[pl.BlockSpec(memory_space=pltpu.SMEM), vmem, vmem],
            out_specs=vmem,
            scratch_shapes=[
                pltpu.VMEM((ROUNDS, 5, rows, values), jnp.bfloat16),
                pltpu.VMEM((rows, values), jnp.float32),
                pltpu.VMEM((rows, points), jnp.float32),
                pltpu.VMEM((rows, points), jnp.float32),
                pltpu.VMEM((leaves, GROUP * points), jnp.float32),
                pltpu.VMEM((5, leaves, rows), jnp.float32),
                pltpu.VMEM((4, leaves, 128), jnp.float32),
                pltpu.SemaphoreType.DMA((ROUNDS, 5, CHUNKS)),
                pltpu.SemaphoreType.DMA((ROUNDS, 5, CHUNKS)),
                pltpu.SemaphoreType.DMA((2,)),
                pltpu.SemaphoreType.DMA((2,)),
            ],
            compiler_params=pltpu.CompilerParams(
                collective_id=0, has_side_effects=True, vmem_limit_bytes=56 << 20
            ),
            name="denoise",
        )(pair_count, pair_leaves, patches.reshape(rows, values))
        return out.reshape(leaves, points, values)

    return jax.shard_map(
        on_device,
        mesh=mesh,
        in_specs=(P(("gz", "xy"), None, None), P(("gz", "xy"), None), P()),
        out_specs=P(("gz", "xy"), None, None),
        check_vma=False,
    )
```

```python
import functools
import math

import jax
import jax.numpy as jnp
from jax import lax
from jax.experimental import pallas as pl
from jax.experimental.pallas import tpu as pltpu
from jax.sharding import PartitionSpec as P

MESH = pl.DeviceIdType.MESH
ROUNDS = 2
RING = 4
PIECES = 8
BATCH = 2
HALF = PIECES // 2
PART = 2
OWN, RIGHT, LEFT, ACROSS, SIDE_A, SIDE_B, TRANSIT = range(7)
STAY, NEXT, PREV, NEXT2, PREV2 = range(5)
FIRST_AT = (2, 2, 1, 2, 1, 1, 1, 2, 8)
FIRST = (
    ((OWN, 0), (OWN, 1)), ((OWN, 2), (OWN, 3)), ((RIGHT, 4), (OWN, 4)), ((OWN, 5), (OWN, 6)),
    ((RIGHT, 5), (SIDE_A, 0)), ((ACROSS, 0), (ACROSS, 4)), ((SIDE_A, 1), (OWN, 7)), ((ACROSS, 1), (ACROSS, 5)),
    ((SIDE_B, 0), (RIGHT, 6)), ((SIDE_B, 4), (RIGHT, 7)), ((SIDE_B, 1), (ACROSS, 2)), ((ACROSS, 6), (SIDE_B, 5)),
    ((ACROSS, 3), (ACROSS, 7)), ((SIDE_A, 2), (RIGHT, 0)), ((SIDE_A, 4), (SIDE_A, 3)), ((RIGHT, 1), (SIDE_A, 5)),
    ((SIDE_B, 2), (RIGHT, 2)), ((SIDE_A, 6), (SIDE_B, 6)), ((RIGHT, 3), (SIDE_A, 7)), ((SIDE_B, 3), (SIDE_B, 7)),
)
INNER_AT = (2, 2, 2, 1, 1, 2, 1, 2, 7)
INNER = (
    ((OWN, 0), (OWN, 1)), ((OWN, 2), (OWN, 3)), ((RIGHT, 4), (LEFT, 0)), ((OWN, 4), (OWN, 5)),
    ((RIGHT, 5), (LEFT, 1)), ((OWN, 6), (OWN, 7)), ((ACROSS, 0), (ACROSS, 4)), ((ACROSS, 1), (ACROSS, 5)),
    ((SIDE_A, 0), (RIGHT, 6)), ((LEFT, 2), (SIDE_A, 4)), ((RIGHT, 7), (LEFT, 3)), ((SIDE_A, 1), (ACROSS, 2)),
    ((ACROSS, 6), (SIDE_A, 5)), ((ACROSS, 3), (ACROSS, 7)), ((SIDE_A, 2), (RIGHT, 0)), ((LEFT, 4), (SIDE_A, 6)),
    ((RIGHT, 1), (LEFT, 5)), ((SIDE_A, 3), (RIGHT, 2)), ((LEFT, 6), (SIDE_A, 7)), ((RIGHT, 3), (LEFT, 7)),
)
LAST_AT = FIRST_AT
LAST = tuple(
    tuple(
        (LEFT if block == RIGHT else block, part if block == OWN else (part + 4) % 8)
        for block, part in unit
    )
    for unit in FIRST
)


def chosen(values, index):
    result = values[0]
    for k in range(1, len(values)):
        if values[k] is not values[0]:
            result = jnp.where(index == k, values[k], result)
    return result


def split(square):
    high = square.astype(jnp.bfloat16)
    low = (square - high.astype(jnp.float32)).astype(jnp.bfloat16)
    return high, low


def squares(block):
    wide = block.astype(jnp.float32)
    return split(wide * wide)


def contract(a, b, da, db):
    return lax.dot_general(
        a, b, (((da,), (db,)), ((), ())), preferred_element_type=jnp.float32
    )


def kernel(
    shape,
    sizes,
    count_ref,
    pairs_ref,
    patches_ref,
    out_ref,
    window,
    numer,
    denom,
    target_power,
    source_row,
    extra,
    listed,
    block_send,
    block_recv,
    listed_send,
    listed_recv,
):
    outer, inner = shape
    leaves, points = sizes
    devices = outer * inner
    rows = leaves * points
    chunk = rows // PIECES
    width = PART * points
    parts_here = leaves // PART
    per_part = PIECES // parts_here
    spread = patches_ref.shape[1] / 4.0
    scale = math.log2(math.e) / spread
    me = lax.axis_index("gz") * inner + lax.axis_index("xy")
    row, z = me // RING, lax.rem(me, RING)

    def device(step):
        index = lax.rem(me + step + devices, devices)
        return (index // inner, lax.rem(index, inner))

    def along(step):
        index = row * RING + lax.rem(z + step + RING, RING)
        return (index // inner, lax.rem(index, inner))

    right, left = along(1), along(-1)
    up, down = device(RING), device(-RING)
    first, last = z == 0, z == RING - 1
    edge = first | last
    toward = lax.rem(me + jnp.where(z < 2, RING, -RING) + devices, devices)
    over = (toward // inner, lax.rem(toward, inner))

    barrier = pltpu.get_barrier_semaphore()
    peers = (right, left, up, down, device(1), device(-1), device(2), device(-2))
    for peer in peers:
        pl.semaphore_signal(barrier, inc=1, device_id=peer, device_id_type=MESH)

    def moved(turn, flow, source, slot, piece, target):
        place = pl.ds(pl.multiple_of(piece * chunk, chunk), chunk)
        return pltpu.make_async_remote_copy(
            src_ref=window.at[turn, source, place],
            dst_ref=window.at[turn, slot, place],
            send_sem=block_send.at[turn, flow, piece],
            recv_sem=block_recv.at[turn, slot, piece],
            device_id=target,
            device_id_type=MESH,
        )

    def arrived(turn, slot, piece):
        moved(turn, 0, OWN, slot, piece, right).wait_recv()

    def start(copy):
        copy.start()

    def finish_send(copy):
        copy.wait_send()

    def own_copies(turn, order, act):
        @pl.when((order < HALF) | jnp.logical_not(last))
        def _():
            act(moved(turn, 0, OWN, LEFT, order, right))

        @pl.when((order < HALF) | jnp.logical_not(first))
        def _():
            act(moved(turn, 1, OWN, RIGHT, lax.rem(order + HALF, PIECES), left))

    def transit_copies(turn, order, act):
        @pl.when(first)
        def _():
            act(moved(turn, 2, OWN, TRANSIT, order, down))

        @pl.when(last)
        def _():
            act(moved(turn, 2, OWN, TRANSIT, HALF + order, up))

    def ring_copies(turn, order, act):
        act(moved(turn, 3, LEFT, ACROSS, order, right))
        act(moved(turn, 3, RIGHT, ACROSS, HALF + order, left))

    def edge_copies(turn, order, act):
        @pl.when(first)
        def _():
            act(moved(turn, 4, LEFT, SIDE_A, order, up))

        @pl.when(last)
        def _():
            act(moved(turn, 4, RIGHT, SIDE_A, HALF + order, down))

    def over_copies(turn, order, act):
        for piece in (order, HALF + order):

            @pl.when(edge)
            def _():
                act(moved(turn, 5, ACROSS, SIDE_B, piece, over))

            @pl.when(jnp.logical_not(edge))
            def _():
                act(moved(turn, 5, ACROSS, SIDE_A, piece, over))

    def onward_copies(turn, order, act):
        @pl.when(first)
        def _():
            act(moved(turn, 6, TRANSIT, SIDE_A, order, left))

        @pl.when(last)
        def _():
            act(moved(turn, 6, TRANSIT, SIDE_A, HALF + order, right))

    def send_rest(turn, order):
        own_copies(turn, order, start)

        @pl.when(order >= HALF)
        def _():
            later = order - HALF

            @pl.when(first)
            def _():
                arrived(turn, TRANSIT, later)

            @pl.when(last)
            def _():
                arrived(turn, TRANSIT, order)

            onward_copies(turn, later, start)

    def transfers(turn, at):
        batch, place = (at - 1) // (2 * BATCH), lax.rem(at - 1, 2 * BATCH)
        order = BATCH * batch + lax.rem(place, BATCH)

        @pl.when((at > 0) & (place < BATCH))
        def _():
            arrived(turn, LEFT, order)
            arrived(turn, RIGHT, HALF + order)
            ring_copies(turn, order, start)
            edge_copies(turn, order, start)

        @pl.when((at > 0) & (place >= BATCH))
        def _():
            send_rest(turn, order + BATCH)
            arrived(turn, ACROSS, order)
            arrived(turn, ACROSS, HALF + order)
            over_copies(turn, order, start)

        @pl.when(at == PIECES)
        def _():
            for later in range(BATCH, HALF):
                send_rest(turn, HALF + later)

    window[0, OWN] = patches_ref[...]
    pl.semaphore_wait(barrier, len(peers))
    for order in range(BATCH):
        own_copies(0, order, start)

    def send_transit(order, _):
        transit_copies(0, order, start)
        return 0

    lax.fori_loop(0, HALF, send_transit, 0)

    slots = pairs_ref.shape[1]
    lanes = 128
    leaf = lax.broadcasted_iota(jnp.int32, (lanes, slots), 0) + me * leaves
    live = lax.broadcasted_iota(jnp.int32, (lanes, slots), 1) < count_ref[me]
    one_a = jnp.where(live & (pairs_ref[0:1, :] == leaf), 1.0, 0.0).astype(jnp.bfloat16)
    one_b = jnp.where(live & (pairs_ref[1:2, :] == leaf), 1.0, 0.0).astype(jnp.bfloat16)
    forward = contract(one_a, one_b, 1, 1)
    backward = contract(one_b, one_a, 1, 1)
    listed[0] = backward[leaves : 2 * leaves]
    listed[1] = backward[2 * leaves : 3 * leaves]

    def listed_copy(k):
        return pltpu.make_async_remote_copy(
            src_ref=listed.at[k],
            dst_ref=listed.at[2 + k],
            send_sem=listed_send.at[k],
            recv_sem=listed_recv.at[k],
            device_id=device(k + 1),
            device_id_type=MESH,
        )

    for k in range(2):
        listed_copy(k).start()

    def expand(counts, base):
        place = lax.broadcasted_iota(jnp.int32, (lanes, rows), 0) - base
        at = lax.broadcasted_iota(jnp.int32, (lanes, rows), 1) - place * points
        spots = jnp.where((at >= 0) & (at < points), 1.0, 0.0).astype(jnp.bfloat16)
        wide = contract(counts.astype(jnp.bfloat16), spots, 1, 0)
        return jnp.where(wide > 0.0, jnp.log2(wide), -jnp.inf)

    ahead = forward[:leaves]
    extra[STAY] = expand(ahead + backward[:leaves], 0)
    extra[NEXT] = expand(ahead, leaves)
    extra[NEXT2] = expand(ahead, 2 * leaves)
    for k in range(2):
        listed_copy(k).wait()
    extra[PREV] = expand(listed[2], 0)
    extra[PREV2] = expand(listed[3], 0)

    def unit(turn, number):
        sources, rows_here = [], []
        for half in range(2):
            codes = [
                jnp.where(
                    first,
                    8 * f[half][0] + f[half][1],
                    jnp.where(last, 8 * l[half][0] + l[half][1], 8 * i[half][0] + i[half][1]),
                )
                for f, i, l in zip(FIRST, INNER, LAST)
            ]
            code = chosen(codes, number)
            slot, part = code // 8, lax.rem(code, 8)
            side = (slot == SIDE_A) | (slot == SIDE_B)
            late = ((slot == LEFT) & (part >= 4)) | ((slot == RIGHT) & (part < 4))

            @pl.when(side | late)
            def _():
                for k in range(per_part):
                    arrived(turn, slot, part * per_part + k)

            near = jnp.where(first, PREV, jnp.where(z == 1, PREV2, jnp.where(last, NEXT, NEXT2)))
            far = jnp.where(z < 2, NEXT2, PREV2)
            beyond = jnp.where(first, PREV2, NEXT2)
            step = chosen((STAY, NEXT, PREV, far, near, beyond), slot)
            place = pl.ds(pl.multiple_of(part * width, width), width)
            sources.append(window[turn, slot, place, :])
            rows_here.append(extra[step, :, place])
        source = jnp.concatenate(sources, axis=0)
        high, low = squares(source)
        ones = jnp.ones((8, source.shape[1]), jnp.bfloat16)
        power = contract(ones, high, 1, 1) + contract(ones, low, 1, 1)
        source_row[...] = power[0:1] * scale - jnp.concatenate(rows_here, axis=1)
        cross = contract(window[turn, OWN], source, 1, 1)
        parts = []
        for t in range(leaves):
            span = slice(t * points, (t + 1) * points)
            total, part = None, []
            for s in range(2 * PART):
                lanes_here = slice(s * points, (s + 1) * points)
                away = target_power[span, :] + source_row[t : t + 1, lanes_here]
                weight = jnp.exp2(cross[span, lanes_here] * (2.0 * scale) - away)
                total = weight if total is None else total + weight
                part.append(weight.astype(jnp.bfloat16))
            denom[span, :] += total
            parts.append(jnp.concatenate(part, axis=1))
        weights = jnp.concatenate(parts, axis=0)
        numer[...] += jnp.dot(weights, source, preferred_element_type=jnp.float32)

    def one_round(turn, _):
        high, low = squares(window[turn, OWN])
        ones = jnp.ones((high.shape[1], points), jnp.bfloat16)
        target_power[...] = scale * (contract(high, ones, 1, 0) + contract(low, ones, 1, 0))
        numer[...] = jnp.zeros_like(numer)
        denom[...] = jnp.zeros_like(denom)

        def step(at, done):
            transfers(turn, at)
            more = chosen(
                [
                    jnp.where(first | last, e, i) if e != i else e
                    for e, i in zip(FIRST_AT, INNER_AT)
                ],
                at,
            )

            def each(k, _):
                unit(turn, done + k)
                return 0

            lax.fori_loop(0, more, each, 0)
            return done + more

        lax.fori_loop(0, len(FIRST_AT), step, 0)

        def finish(order, _):
            piece = order // 2 + HALF * lax.rem(order, 2)
            place = pl.ds(pl.multiple_of(piece * chunk, chunk), chunk)
            below = 1.0 + jnp.sum(denom[place, :], axis=1, keepdims=True)
            above = window[turn, OWN, place, :].astype(jnp.float32) + numer[place, :]
            out_ref[place, :] = (above * (1.0 / below)).astype(jnp.bfloat16)

            @pl.when(turn + 1 < ROUNDS)
            def _():
                window[1, OWN, place, :] = out_ref[place, :]

                @pl.when((lax.rem(order, 2) == 1) & (order // 2 < BATCH))
                def _():
                    own_copies(1, order // 2, start)

                @pl.when(lax.rem(order, 2) == 1)
                def _():
                    transit_copies(1, order // 2, start)

            return 0

        lax.fori_loop(0, PIECES, finish, 0)
        return 0

    lax.fori_loop(0, ROUNDS, one_round, 0)

    def drain(order, _):
        for turn in range(ROUNDS):
            own_copies(turn, order, finish_send)
            own_copies(turn, HALF + order, finish_send)
            for kind in (
                transit_copies,
                ring_copies,
                edge_copies,
                over_copies,
                onward_copies,
            ):
                kind(turn, order, finish_send)
        return 0

    lax.fori_loop(0, HALF, drain, 0)


def solution(mesh):
    shape = (mesh.shape["gz"], mesh.shape["xy"])

    def on_device(patches, pair_leaves, pair_count):
        leaves, points, values = patches.shape
        rows = leaves * points
        vmem = pl.BlockSpec(memory_space=pltpu.VMEM)
        out = pl.pallas_call(
            functools.partial(kernel, shape, (leaves, points)),
            out_shape=jax.ShapeDtypeStruct((rows, values), jnp.bfloat16),
            in_specs=[pl.BlockSpec(memory_space=pltpu.SMEM), vmem, vmem],
            out_specs=vmem,
            scratch_shapes=[
                pltpu.VMEM((ROUNDS, 7, rows, values), jnp.bfloat16),
                pltpu.VMEM((rows, values), jnp.float32),
                pltpu.VMEM((rows, points), jnp.float32),
                pltpu.VMEM((rows, points), jnp.float32),
                pltpu.VMEM((leaves, 2 * PART * points), jnp.float32),
                pltpu.VMEM((5, leaves, rows), jnp.float32),
                pltpu.VMEM((4, leaves, 128), jnp.float32),
                pltpu.SemaphoreType.DMA((ROUNDS, 7, PIECES)),
                pltpu.SemaphoreType.DMA((ROUNDS, 7, PIECES)),
                pltpu.SemaphoreType.DMA((2,)),
                pltpu.SemaphoreType.DMA((2,)),
            ],
            compiler_params=pltpu.CompilerParams(
                collective_id=0, has_side_effects=True, vmem_limit_bytes=56 << 20
            ),
            name="denoise",
        )(pair_count, pair_leaves.T, patches.reshape(rows, values))
        return out.reshape(leaves, points, values)

    return jax.shard_map(
        on_device,
        mesh=mesh,
        in_specs=(P(("gz", "xy"), None, None), P(("gz", "xy"), None), P()),
        out_specs=P(("gz", "xy"), None, None),
        check_vma=False,
    )
```

```python
import functools
import math

import jax
import jax.numpy as jnp
from jax import lax
from jax.experimental import pallas as pl
from jax.experimental.pallas import tpu as pltpu
from jax.sharding import PartitionSpec as P

MESH = pl.DeviceIdType.MESH
ROUNDS = 2
RING = 4
PIECES = 8
BATCH = 2
SHIFT = 1
HALF = PIECES // 2
PART = 2
OWN, RIGHT, LEFT, ACROSS, SIDE_A, SIDE_B, TRANSIT = range(7)
STAY, NEXT, PREV, NEXT2, PREV2 = range(5)
FIRST_AT = (1, 2, 2, 1, 2, 1, 1, 1, 9)
FIRST = (
    ((OWN, 0), (OWN, 1)), ((RIGHT, 4), (OWN, 2)), ((OWN, 3), (OWN, 4)), ((RIGHT, 5), (OWN, 5)),
    ((OWN, 6), (OWN, 7)), ((SIDE_A, 0), (ACROSS, 0)), ((ACROSS, 4), (SIDE_A, 1)), ((ACROSS, 1), (ACROSS, 5)),
    ((RIGHT, 6), (SIDE_B, 0)), ((RIGHT, 7), (SIDE_B, 4)), ((ACROSS, 6), (SIDE_B, 1)), ((ACROSS, 2), (ACROSS, 7)),
    ((SIDE_B, 5), (ACROSS, 3)), ((RIGHT, 0), (SIDE_A, 2)), ((SIDE_A, 4), (RIGHT, 1)), ((SIDE_B, 2), (SIDE_A, 5)),
    ((RIGHT, 2), (SIDE_B, 6)), ((SIDE_A, 6), (RIGHT, 3)), ((SIDE_B, 3), (SIDE_A, 7)), ((SIDE_B, 7), (SIDE_A, 3)),
)
INNER_AT = (1, 2, 2, 1, 2, 1, 2, 2, 7)
INNER = (
    ((OWN, 0), (OWN, 1)), ((LEFT, 0), (RIGHT, 4)), ((OWN, 2), (OWN, 3)), ((LEFT, 1), (RIGHT, 5)),
    ((OWN, 4), (OWN, 5)), ((ACROSS, 0), (ACROSS, 4)), ((ACROSS, 1), (ACROSS, 5)), ((OWN, 6), (OWN, 7)),
    ((SIDE_A, 0), (LEFT, 2)), ((RIGHT, 6), (SIDE_A, 4)), ((RIGHT, 7), (LEFT, 3)), ((SIDE_A, 1), (ACROSS, 6)),
    ((ACROSS, 2), (SIDE_A, 5)), ((ACROSS, 7), (ACROSS, 3)), ((SIDE_A, 2), (RIGHT, 0)), ((LEFT, 4), (SIDE_A, 6)),
    ((RIGHT, 1), (LEFT, 5)), ((SIDE_A, 3), (RIGHT, 2)), ((LEFT, 6), (SIDE_A, 7)), ((RIGHT, 3), (LEFT, 7)),
)
LAST_AT = FIRST_AT
LAST = tuple(
    tuple(
        (LEFT if block == RIGHT else block, part if block == OWN else (part + 4) % 8)
        for block, part in unit
    )
    for unit in FIRST
)


def chosen(values, index):
    result = values[0]
    for k in range(1, len(values)):
        if values[k] is not values[0]:
            result = jnp.where(index == k, values[k], result)
    return result


def split(square):
    high = square.astype(jnp.bfloat16)
    low = (square - high.astype(jnp.float32)).astype(jnp.bfloat16)
    return high, low


def squares(block):
    wide = block.astype(jnp.float32)
    return split(wide * wide)


def contract(a, b, da, db):
    return lax.dot_general(
        a, b, (((da,), (db,)), ((), ())), preferred_element_type=jnp.float32
    )


def kernel(
    shape,
    sizes,
    count_ref,
    pairs_ref,
    patches_ref,
    out_ref,
    window,
    numer,
    denom,
    target_power,
    source_row,
    extra,
    listed,
    block_send,
    block_recv,
    listed_send,
    listed_recv,
):
    outer, inner = shape
    leaves, points = sizes
    devices = outer * inner
    rows = leaves * points
    chunk = rows // PIECES
    width = PART * points
    parts_here = leaves // PART
    per_part = PIECES // parts_here
    spread = patches_ref.shape[1] / 4.0
    scale = math.log2(math.e) / spread
    me = lax.axis_index("gz") * inner + lax.axis_index("xy")
    row, z = me // RING, lax.rem(me, RING)

    def device(step):
        index = lax.rem(me + step + devices, devices)
        return (index // inner, lax.rem(index, inner))

    def along(step):
        index = row * RING + lax.rem(z + step + RING, RING)
        return (index // inner, lax.rem(index, inner))

    right, left = along(1), along(-1)
    up, down = device(RING), device(-RING)
    first, last = z == 0, z == RING - 1
    edge = first | last
    toward = lax.rem(me + jnp.where(z < 2, RING, -RING) + devices, devices)
    over = (toward // inner, lax.rem(toward, inner))

    barrier = pltpu.get_barrier_semaphore()
    peers = (right, left, up, down, device(1), device(-1), device(2), device(-2))
    for peer in peers:
        pl.semaphore_signal(barrier, inc=1, device_id=peer, device_id_type=MESH)

    def moved(turn, flow, source, slot, piece, target):
        place = pl.ds(pl.multiple_of(piece * chunk, chunk), chunk)
        return pltpu.make_async_remote_copy(
            src_ref=window.at[turn, source, place],
            dst_ref=window.at[turn, slot, place],
            send_sem=block_send.at[turn, flow, piece],
            recv_sem=block_recv.at[turn, slot, piece],
            device_id=target,
            device_id_type=MESH,
        )

    def arrived(turn, slot, piece):
        moved(turn, 0, OWN, slot, piece, right).wait_recv()

    def start(copy):
        copy.start()

    def finish_send(copy):
        copy.wait_send()

    def own_copies(turn, order, act):
        @pl.when((order < HALF) | jnp.logical_not(last))
        def _():
            act(moved(turn, 0, OWN, LEFT, order, right))

        @pl.when((order < HALF) | jnp.logical_not(first))
        def _():
            act(moved(turn, 1, OWN, RIGHT, lax.rem(order + HALF, PIECES), left))

    def passing(order):
        at_last = jnp.where(order < HALF, HALF + order, order - SHIFT)
        return lax.rem(at_last + HALF, PIECES), at_last

    def transit_copies(turn, order, act):
        at_first, at_last = passing(order)

        @pl.when(first)
        def _():
            act(moved(turn, 2, OWN, TRANSIT, at_first, down))

        @pl.when(last)
        def _():
            act(moved(turn, 2, OWN, TRANSIT, at_last, up))

    def ring_copies(turn, order, act):
        act(moved(turn, 3, LEFT, ACROSS, order, right))
        act(moved(turn, 3, RIGHT, ACROSS, HALF + order, left))

    def edge_copies(turn, order, act):
        @pl.when(first & (order < HALF - SHIFT))
        def _():
            act(moved(turn, 4, LEFT, SIDE_A, order, up))

        @pl.when(last & (order < HALF - SHIFT))
        def _():
            act(moved(turn, 4, RIGHT, SIDE_A, HALF + order, down))

    def over_copies(turn, order, act):
        for piece in (order, HALF + order):

            @pl.when(edge)
            def _():
                act(moved(turn, 5, ACROSS, SIDE_B, piece, over))

            @pl.when(jnp.logical_not(edge))
            def _():
                act(moved(turn, 5, ACROSS, SIDE_A, piece, over))

    def onward_copies(turn, order, act):
        at_first, at_last = passing(order)

        @pl.when(first)
        def _():
            act(moved(turn, 6, TRANSIT, SIDE_A, at_first, left))

        @pl.when(last)
        def _():
            act(moved(turn, 6, TRANSIT, SIDE_A, at_last, right))

    def pass_on(turn, order):
        at_first, at_last = passing(order)

        @pl.when(first)
        def _():
            arrived(turn, TRANSIT, at_first)

        @pl.when(last)
        def _():
            arrived(turn, TRANSIT, at_last)

        onward_copies(turn, order, start)

    def send_rest(turn, order):
        own_copies(turn, order, start)

        @pl.when(order >= HALF)
        def _():
            pass_on(turn, order - HALF)

    def transfers(turn, at):
        batch, place = (at - 1) // (2 * BATCH), lax.rem(at - 1, 2 * BATCH)
        order = BATCH * batch + lax.rem(place, BATCH)

        @pl.when((at > 0) & (place < BATCH))
        def _():
            arrived(turn, LEFT, order)
            arrived(turn, RIGHT, HALF + order)
            ring_copies(turn, order, start)
            edge_copies(turn, order, start)

        @pl.when((at > 0) & (place >= BATCH))
        def _():
            send_rest(turn, order + BATCH)
            arrived(turn, ACROSS, order)
            arrived(turn, ACROSS, HALF + order)
            over_copies(turn, order, start)

        @pl.when(at == PIECES)
        def _():
            for later in range(BATCH, HALF):
                send_rest(turn, HALF + later)
            for later in range(SHIFT):
                pass_on(turn, HALF + later)

    window[0, OWN] = patches_ref[...]
    pl.semaphore_wait(barrier, len(peers))
    for order in range(BATCH):
        own_copies(0, order, start)

    def send_transit(order, _):
        transit_copies(0, order, start)
        return 0

    lax.fori_loop(0, HALF + SHIFT, send_transit, 0)

    slots = pairs_ref.shape[1]
    lanes = 128
    leaf = lax.broadcasted_iota(jnp.int32, (lanes, slots), 0) + me * leaves
    live = lax.broadcasted_iota(jnp.int32, (lanes, slots), 1) < count_ref[me]
    one_a = jnp.where(live & (pairs_ref[0:1, :] == leaf), 1.0, 0.0).astype(jnp.bfloat16)
    one_b = jnp.where(live & (pairs_ref[1:2, :] == leaf), 1.0, 0.0).astype(jnp.bfloat16)
    forward = contract(one_a, one_b, 1, 1)
    backward = contract(one_b, one_a, 1, 1)
    listed[0] = backward[leaves : 2 * leaves]
    listed[1] = backward[2 * leaves : 3 * leaves]

    def listed_copy(k):
        return pltpu.make_async_remote_copy(
            src_ref=listed.at[k],
            dst_ref=listed.at[2 + k],
            send_sem=listed_send.at[k],
            recv_sem=listed_recv.at[k],
            device_id=device(k + 1),
            device_id_type=MESH,
        )

    for k in range(2):
        listed_copy(k).start()

    def begin_round(turn):
        high, low = squares(window[turn, OWN])
        ones = jnp.ones((high.shape[1], points), jnp.bfloat16)
        target_power[...] = scale * (contract(high, ones, 1, 0) + contract(low, ones, 1, 0))
        numer[...] = jnp.zeros_like(numer)
        denom[...] = jnp.zeros_like(denom)

    begin_round(0)
    ahead = forward[:leaves]
    for k in range(2):
        listed_copy(k).wait()
    counts = jnp.concatenate(
        [
            ahead + backward[:leaves],
            pltpu.roll(ahead, lanes - leaves, 1),
            listed[2],
            pltpu.roll(ahead, lanes - 2 * leaves, 1),
            listed[3],
        ],
        axis=0,
    )
    place = lax.broadcasted_iota(jnp.int32, (lanes, rows), 0)
    at = lax.broadcasted_iota(jnp.int32, (lanes, rows), 1) - place * points
    spots = jnp.where((at >= 0) & (at < points), 1.0, 0.0).astype(jnp.bfloat16)
    wide = contract(counts.astype(jnp.bfloat16), spots, 1, 0)
    wide = jnp.where(wide > 0.0, jnp.log2(wide), -jnp.inf)
    for k in range(5):
        extra[k] = wide[k * leaves : (k + 1) * leaves]

    def unit(turn, number):
        sources, rows_here = [], []
        for half in range(2):
            codes = [
                jnp.where(
                    first,
                    8 * f[half][0] + f[half][1],
                    jnp.where(last, 8 * l[half][0] + l[half][1], 8 * i[half][0] + i[half][1]),
                )
                for f, i, l in zip(FIRST, INNER, LAST)
            ]
            code = chosen(codes, number)
            slot, part = code // 8, lax.rem(code, 8)
            side = (slot == SIDE_A) | (slot == SIDE_B)
            late = ((slot == LEFT) & (part >= 4)) | ((slot == RIGHT) & (part < 4))

            @pl.when(side | late)
            def _():
                for k in range(per_part):
                    arrived(turn, slot, part * per_part + k)

            near = jnp.where(first, PREV, jnp.where(z == 1, PREV2, jnp.where(last, NEXT, NEXT2)))
            far = jnp.where(z < 2, NEXT2, PREV2)
            beyond = jnp.where(first, PREV2, NEXT2)
            step = chosen((STAY, NEXT, PREV, far, near, beyond), slot)
            place = pl.ds(pl.multiple_of(part * width, width), width)
            sources.append(window[turn, slot, place, :])
            rows_here.append(extra[step, :, place])
        source = jnp.concatenate(sources, axis=0)
        wide = source.astype(jnp.float32)
        wide = wide * wide
        folded = wide[:, :points] + wide[:, points:]
        power = [
            jnp.sum(folded[s * points : (s + 1) * points].T, axis=0, keepdims=True)
            for s in range(2 * PART)
        ]
        source_row[...] = jnp.concatenate(power, axis=1) * scale - jnp.concatenate(
            rows_here, axis=1
        )
        cross = contract(window[turn, OWN], source, 1, 1)
        parts = []
        for t in range(leaves):
            span = slice(t * points, (t + 1) * points)
            total, part = None, []
            for s in range(2 * PART):
                lanes_here = slice(s * points, (s + 1) * points)
                away = target_power[span, :] + source_row[t : t + 1, lanes_here]
                weight = jnp.exp2(cross[span, lanes_here] * (2.0 * scale) - away)
                total = weight if total is None else total + weight
                part.append(weight.astype(jnp.bfloat16))
            denom[span, :] += total
            parts.append(jnp.concatenate(part, axis=1))
        weights = jnp.concatenate(parts, axis=0)
        numer[...] += jnp.dot(weights, source, preferred_element_type=jnp.float32)

    def one_round(turn, _):
        @pl.when(turn > 0)
        def _():
            begin_round(turn)

        def step(at, done):
            transfers(turn, at)
            more = chosen(
                [
                    jnp.where(first | last, e, i) if e != i else e
                    for e, i in zip(FIRST_AT, INNER_AT)
                ],
                at,
            )

            def each(k, _):
                unit(turn, done + k)
                return 0

            lax.fori_loop(0, more, each, 0)
            return done + more

        lax.fori_loop(0, len(FIRST_AT), step, 0)

        def finish(order, _):
            piece = order // 2 + HALF * lax.rem(order, 2)
            place = pl.ds(pl.multiple_of(piece * chunk, chunk), chunk)
            below = 1.0 + jnp.sum(denom[place, :], axis=1, keepdims=True)
            above = window[turn, OWN, place, :].astype(jnp.float32) + numer[place, :]
            out_ref[place, :] = (above * (1.0 / below)).astype(jnp.bfloat16)

            @pl.when(turn + 1 < ROUNDS)
            def _():
                window[1, OWN, place, :] = out_ref[place, :]

                @pl.when((lax.rem(order, 2) == 1) & (order // 2 < BATCH))
                def _():
                    own_copies(1, order // 2, start)

                @pl.when(lax.rem(order, 2) == 1)
                def _():
                    transit_copies(1, order // 2, start)

                @pl.when(order == PIECES - 1)
                def _():
                    for later in range(SHIFT):
                        transit_copies(1, HALF + later, start)

            return 0

        lax.fori_loop(0, PIECES, finish, 0)
        return 0

    lax.fori_loop(0, ROUNDS, one_round, 0)

    def drain(order, _):
        for turn in range(ROUNDS):
            own_copies(turn, order, finish_send)
            own_copies(turn, HALF + order, finish_send)
            for kind in (
                transit_copies,
                ring_copies,
                edge_copies,
                over_copies,
                onward_copies,
            ):
                kind(turn, order, finish_send)
        return 0

    lax.fori_loop(0, HALF, drain, 0)
    for turn in range(ROUNDS):
        for order in range(HALF, HALF + SHIFT):
            transit_copies(turn, order, finish_send)
            onward_copies(turn, order, finish_send)


def solution(mesh):
    shape = (mesh.shape["gz"], mesh.shape["xy"])

    def on_device(patches, pair_leaves, pair_count):
        leaves, points, values = patches.shape
        rows = leaves * points
        vmem = pl.BlockSpec(memory_space=pltpu.VMEM)
        out = pl.pallas_call(
            functools.partial(kernel, shape, (leaves, points)),
            out_shape=jax.ShapeDtypeStruct((rows, values), jnp.bfloat16),
            in_specs=[pl.BlockSpec(memory_space=pltpu.SMEM), vmem, vmem],
            out_specs=vmem,
            scratch_shapes=[
                pltpu.VMEM((ROUNDS, 7, rows, values), jnp.bfloat16),
                pltpu.VMEM((rows, values), jnp.float32),
                pltpu.VMEM((rows, points), jnp.float32),
                pltpu.VMEM((rows, points), jnp.float32),
                pltpu.VMEM((leaves, 2 * PART * points), jnp.float32),
                pltpu.VMEM((5, leaves, rows), jnp.float32),
                pltpu.VMEM((4, leaves, 128), jnp.float32),
                pltpu.SemaphoreType.DMA((ROUNDS, 7, PIECES)),
                pltpu.SemaphoreType.DMA((ROUNDS, 7, PIECES)),
                pltpu.SemaphoreType.DMA((2,)),
                pltpu.SemaphoreType.DMA((2,)),
            ],
            compiler_params=pltpu.CompilerParams(
                collective_id=0, has_side_effects=True, vmem_limit_bytes=56 << 20
            ),
            name="denoise",
        )(pair_count, pair_leaves.T, patches.reshape(rows, values))
        return out.reshape(leaves, points, values)

    return jax.shard_map(
        on_device,
        mesh=mesh,
        in_specs=(P(("gz", "xy"), None, None), P(("gz", "xy"), None), P()),
        out_specs=P(("gz", "xy"), None, None),
        check_vma=False,
    )
```

```python
import functools
import math

import jax
import jax.numpy as jnp
from jax import lax
from jax.experimental import pallas as pl
from jax.experimental.pallas import tpu as pltpu
from jax.sharding import PartitionSpec as P

MESH = pl.DeviceIdType.MESH
ROUNDS = 2
RING = 4
PIECES = 8
BATCH = 2
SHIFT = 1
HALF = PIECES // 2
PART = 2
OWN, RIGHT, LEFT, ACROSS, SIDE_A, SIDE_B, TRANSIT = range(7)
STAY, NEXT, PREV, NEXT2, PREV2 = range(5)
FIRST_AT = (1, 2, 2, 1, 2, 1, 1, 1, 9)
FIRST = (
    ((OWN, 0), (OWN, 1)), ((RIGHT, 4), (OWN, 2)), ((OWN, 3), (OWN, 4)), ((RIGHT, 5), (OWN, 5)),
    ((OWN, 6), (OWN, 7)), ((SIDE_A, 0), (ACROSS, 0)), ((ACROSS, 4), (SIDE_A, 1)), ((ACROSS, 1), (ACROSS, 5)),
    ((RIGHT, 6), (SIDE_B, 0)), ((RIGHT, 7), (SIDE_B, 4)), ((ACROSS, 6), (SIDE_B, 1)), ((ACROSS, 2), (ACROSS, 7)),
    ((SIDE_B, 5), (ACROSS, 3)), ((RIGHT, 0), (SIDE_A, 2)), ((SIDE_A, 4), (RIGHT, 1)), ((SIDE_B, 2), (SIDE_A, 5)),
    ((RIGHT, 2), (SIDE_B, 6)), ((SIDE_A, 6), (RIGHT, 3)), ((SIDE_B, 3), (SIDE_A, 7)), ((SIDE_B, 7), (SIDE_A, 3)),
)
INNER_AT = (1, 2, 2, 1, 2, 1, 2, 2, 7)
INNER = (
    ((OWN, 0), (OWN, 1)), ((LEFT, 0), (RIGHT, 4)), ((OWN, 2), (OWN, 3)), ((LEFT, 1), (RIGHT, 5)),
    ((OWN, 4), (OWN, 5)), ((ACROSS, 0), (ACROSS, 4)), ((ACROSS, 1), (ACROSS, 5)), ((OWN, 6), (OWN, 7)),
    ((SIDE_A, 0), (LEFT, 2)), ((RIGHT, 6), (SIDE_A, 4)), ((RIGHT, 7), (LEFT, 3)), ((SIDE_A, 1), (ACROSS, 6)),
    ((ACROSS, 2), (SIDE_A, 5)), ((ACROSS, 7), (ACROSS, 3)), ((SIDE_A, 2), (RIGHT, 0)), ((LEFT, 4), (SIDE_A, 6)),
    ((RIGHT, 1), (LEFT, 5)), ((SIDE_A, 3), (RIGHT, 2)), ((LEFT, 6), (SIDE_A, 7)), ((RIGHT, 3), (LEFT, 7)),
)
LAST_AT = FIRST_AT
LAST = tuple(
    tuple(
        (LEFT if block == RIGHT else block, part if block == OWN else (part + 4) % 8)
        for block, part in unit
    )
    for unit in FIRST
)


def chosen(values, index):
    result = values[0]
    for k in range(1, len(values)):
        if values[k] is not values[0]:
            result = jnp.where(index == k, values[k], result)
    return result


def split(square):
    high = square.astype(jnp.bfloat16)
    low = (square - high.astype(jnp.float32)).astype(jnp.bfloat16)
    return high, low


def squares(block):
    wide = block.astype(jnp.float32)
    return split(wide * wide)


def contract(a, b, da, db):
    return lax.dot_general(
        a, b, (((da,), (db,)), ((), ())), preferred_element_type=jnp.float32
    )


def kernel(
    shape,
    sizes,
    count_ref,
    pairs_ref,
    patches_ref,
    out_ref,
    window,
    numer,
    denom,
    target_power,
    source_row,
    extra,
    listed,
    result,
    load_sem,
    store_sem,
    block_send,
    block_recv,
    listed_send,
    listed_recv,
):
    outer, inner = shape
    leaves, points = sizes
    devices = outer * inner
    rows = leaves * points
    chunk = rows // PIECES
    width = PART * points
    parts_here = leaves // PART
    per_part = PIECES // parts_here
    spread = patches_ref.shape[1] / 4.0
    scale = math.log2(math.e) / spread
    me = lax.axis_index("gz") * inner + lax.axis_index("xy")
    row, z = me // RING, lax.rem(me, RING)

    def device(step):
        index = lax.rem(me + step + devices, devices)
        return (index // inner, lax.rem(index, inner))

    def along(step):
        index = row * RING + lax.rem(z + step + RING, RING)
        return (index // inner, lax.rem(index, inner))

    right, left = along(1), along(-1)
    up, down = device(RING), device(-RING)
    first, last = z == 0, z == RING - 1
    edge = first | last
    toward = lax.rem(me + jnp.where(z < 2, RING, -RING) + devices, devices)
    over = (toward // inner, lax.rem(toward, inner))

    load = pltpu.make_async_copy(patches_ref, window.at[0, OWN], load_sem)
    load.start()

    barrier = pltpu.get_barrier_semaphore()
    peers = (right, left, up, down, device(1), device(-1), device(2), device(-2))
    for peer in peers:
        pl.semaphore_signal(barrier, inc=1, device_id=peer, device_id_type=MESH)

    def moved(turn, flow, source, slot, piece, target):
        place = pl.ds(pl.multiple_of(piece * chunk, chunk), chunk)
        return pltpu.make_async_remote_copy(
            src_ref=window.at[turn, source, place],
            dst_ref=window.at[turn, slot, place],
            send_sem=block_send.at[turn, flow, piece],
            recv_sem=block_recv.at[turn, slot, piece],
            device_id=target,
            device_id_type=MESH,
        )

    def arrived(turn, slot, piece):
        moved(turn, 0, OWN, slot, piece, right).wait_recv()

    def start(copy):
        copy.start()

    def finish_send(copy):
        copy.wait_send()

    def own_copies(turn, order, act):
        @pl.when((order < HALF) | jnp.logical_not(last))
        def _():
            act(moved(turn, 0, OWN, LEFT, order, right))

        @pl.when((order < HALF) | jnp.logical_not(first))
        def _():
            act(moved(turn, 1, OWN, RIGHT, lax.rem(order + HALF, PIECES), left))

    def passing(order):
        at_last = jnp.where(order < HALF, HALF + order, order - SHIFT)
        return lax.rem(at_last + HALF, PIECES), at_last

    def transit_copies(turn, order, act):
        at_first, at_last = passing(order)

        @pl.when(first)
        def _():
            act(moved(turn, 2, OWN, TRANSIT, at_first, down))

        @pl.when(last)
        def _():
            act(moved(turn, 2, OWN, TRANSIT, at_last, up))

    def ring_copies(turn, order, act):
        act(moved(turn, 3, LEFT, ACROSS, order, right))
        act(moved(turn, 3, RIGHT, ACROSS, HALF + order, left))

    def edge_copies(turn, order, act):
        @pl.when(first & (order < HALF - SHIFT))
        def _():
            act(moved(turn, 4, LEFT, SIDE_A, order, up))

        @pl.when(last & (order < HALF - SHIFT))
        def _():
            act(moved(turn, 4, RIGHT, SIDE_A, HALF + order, down))

    def over_copies(turn, order, act):
        for piece in (order, HALF + order):

            @pl.when(edge)
            def _():
                act(moved(turn, 5, ACROSS, SIDE_B, piece, over))

            @pl.when(jnp.logical_not(edge))
            def _():
                act(moved(turn, 5, ACROSS, SIDE_A, piece, over))

    def onward_copies(turn, order, act):
        at_first, at_last = passing(order)

        @pl.when(first)
        def _():
            act(moved(turn, 6, TRANSIT, SIDE_A, at_first, left))

        @pl.when(last)
        def _():
            act(moved(turn, 6, TRANSIT, SIDE_A, at_last, right))

    def pass_on(turn, order):
        at_first, at_last = passing(order)

        @pl.when(first)
        def _():
            arrived(turn, TRANSIT, at_first)

        @pl.when(last)
        def _():
            arrived(turn, TRANSIT, at_last)

        onward_copies(turn, order, start)

    def send_rest(turn, order):
        own_copies(turn, order, start)

        @pl.when(order >= HALF)
        def _():
            pass_on(turn, order - HALF)

    def transfers(turn, at):
        batch, place = (at - 1) // (2 * BATCH), lax.rem(at - 1, 2 * BATCH)
        order = BATCH * batch + lax.rem(place, BATCH)

        @pl.when((at > 0) & (place < BATCH))
        def _():
            arrived(turn, LEFT, order)
            arrived(turn, RIGHT, HALF + order)
            ring_copies(turn, order, start)
            edge_copies(turn, order, start)

        @pl.when((at > 0) & (place >= BATCH))
        def _():
            send_rest(turn, order + BATCH)
            arrived(turn, ACROSS, order)
            arrived(turn, ACROSS, HALF + order)
            over_copies(turn, order, start)

        @pl.when(at == PIECES)
        def _():
            for later in range(BATCH, HALF):
                send_rest(turn, HALF + later)
            for later in range(SHIFT):
                pass_on(turn, HALF + later)

    pl.semaphore_wait(barrier, len(peers))
    load.wait()
    for order in range(BATCH):
        own_copies(0, order, start)

    def send_transit(order, _):
        transit_copies(0, order, start)
        return 0

    lax.fori_loop(0, HALF + SHIFT, send_transit, 0)

    slots = pairs_ref.shape[1]
    lanes = 128
    leaf = lax.broadcasted_iota(jnp.int32, (lanes, slots), 0) + me * leaves
    live = lax.broadcasted_iota(jnp.int32, (lanes, slots), 1) < count_ref[me]
    one_a = jnp.where(live & (pairs_ref[0:1, :] == leaf), 1.0, 0.0).astype(jnp.bfloat16)
    one_b = jnp.where(live & (pairs_ref[1:2, :] == leaf), 1.0, 0.0).astype(jnp.bfloat16)
    forward = contract(one_a, one_b, 1, 1)
    backward = contract(one_b, one_a, 1, 1)
    listed[0] = backward[leaves : 2 * leaves]
    listed[1] = backward[2 * leaves : 3 * leaves]

    def listed_copy(k):
        return pltpu.make_async_remote_copy(
            src_ref=listed.at[k],
            dst_ref=listed.at[2 + k],
            send_sem=listed_send.at[k],
            recv_sem=listed_recv.at[k],
            device_id=device(k + 1),
            device_id_type=MESH,
        )

    for k in range(2):
        listed_copy(k).start()

    def store(piece):
        place = pl.ds(pl.multiple_of(piece * chunk, chunk), chunk)
        return pltpu.make_async_copy(result.at[place], out_ref.at[place], store_sem.at[piece])

    def begin_round(turn):
        high, low = squares(window[turn, OWN])
        ones = jnp.ones((high.shape[1], points), jnp.bfloat16)
        target_power[...] = scale * (contract(high, ones, 1, 0) + contract(low, ones, 1, 0))
        numer[...] = jnp.zeros_like(numer)
        denom[...] = jnp.zeros_like(denom)

    def tabulate(counts, steps):
        counts = jnp.concatenate(counts, axis=0).astype(jnp.bfloat16)
        place = lax.broadcasted_iota(jnp.int32, (lanes, rows), 0)
        at = lax.broadcasted_iota(jnp.int32, (lanes, rows), 1) - place * points
        spots = jnp.where((at >= 0) & (at < points), 1.0, 0.0).astype(jnp.bfloat16)
        wide = contract(counts, spots, 1, 0)
        wide = jnp.where(wide > 0.0, jnp.log2(wide), -jnp.inf)
        for k, step in enumerate(steps):
            extra[step] = wide[k * leaves : (k + 1) * leaves]

    begin_round(0)
    ahead = forward[:leaves]
    tabulate(
        [
            ahead + backward[:leaves],
            pltpu.roll(ahead, lanes - leaves, 1),
            pltpu.roll(ahead, lanes - 2 * leaves, 1),
        ],
        (STAY, NEXT, NEXT2),
    )

    def unit(turn, number):
        sources, rows_here = [], []
        for half in range(2):
            codes = [
                jnp.where(
                    first,
                    8 * f[half][0] + f[half][1],
                    jnp.where(last, 8 * l[half][0] + l[half][1], 8 * i[half][0] + i[half][1]),
                )
                for f, i, l in zip(FIRST, INNER, LAST)
            ]
            code = chosen(codes, number)
            slot, part = code // 8, lax.rem(code, 8)
            side = (slot == SIDE_A) | (slot == SIDE_B)
            late = ((slot == LEFT) & (part >= 4)) | ((slot == RIGHT) & (part < 4))

            @pl.when(side | late)
            def _():
                for k in range(per_part):
                    arrived(turn, slot, part * per_part + k)

            near = jnp.where(first, PREV, jnp.where(z == 1, PREV2, jnp.where(last, NEXT, NEXT2)))
            far = jnp.where(z < 2, NEXT2, PREV2)
            beyond = jnp.where(first, PREV2, NEXT2)
            step = chosen((STAY, NEXT, PREV, far, near, beyond), slot)
            place = pl.ds(pl.multiple_of(part * width, width), width)
            sources.append(window[turn, slot, place, :])
            rows_here.append(extra[step, :, place])
        source = jnp.concatenate(sources, axis=0)
        wide = source.astype(jnp.float32)
        wide = wide * wide
        folded = wide[:, :points] + wide[:, points:]
        power = [
            jnp.sum(folded[s * points : (s + 1) * points].T, axis=0, keepdims=True)
            for s in range(2 * PART)
        ]
        source_row[...] = jnp.concatenate(power, axis=1) * scale - jnp.concatenate(
            rows_here, axis=1
        )
        cross = contract(window[turn, OWN], source, 1, 1)
        parts = []
        for t in range(leaves):
            span = slice(t * points, (t + 1) * points)
            total, part = None, []
            for s in range(2 * PART):
                lanes_here = slice(s * points, (s + 1) * points)
                away = target_power[span, :] + source_row[t : t + 1, lanes_here]
                weight = jnp.exp2(cross[span, lanes_here] * (2.0 * scale) - away)
                total = weight if total is None else total + weight
                part.append(weight.astype(jnp.bfloat16))
            denom[span, :] += total
            parts.append(jnp.concatenate(part, axis=1))
        weights = jnp.concatenate(parts, axis=0)
        numer[...] += jnp.dot(weights, source, preferred_element_type=jnp.float32)

    def one_round(turn, _):
        @pl.when(turn > 0)
        def _():
            begin_round(turn)

        def step(at, done):
            transfers(turn, at)

            @pl.when((turn == 0) & (at == 1))
            def _():
                for k in range(2):
                    listed_copy(k).wait()
                tabulate([listed[2], listed[3]], (PREV, PREV2))

            more = chosen(
                [
                    jnp.where(first | last, e, i) if e != i else e
                    for e, i in zip(FIRST_AT, INNER_AT)
                ],
                at,
            )

            def each(k, _):
                unit(turn, done + k)
                return 0

            lax.fori_loop(0, more, each, 0)
            return done + more

        lax.fori_loop(0, len(FIRST_AT), step, 0)

        def finish(order, _):
            piece = order // 2 + HALF * lax.rem(order, 2)
            place = pl.ds(pl.multiple_of(piece * chunk, chunk), chunk)
            below = 1.0 + jnp.sum(denom[place, :], axis=1, keepdims=True)
            above = window[turn, OWN, place, :].astype(jnp.float32) + numer[place, :]
            result[place, :] = (above * (1.0 / below)).astype(jnp.bfloat16)

            @pl.when(turn + 1 == ROUNDS)
            def _():
                store(piece).start()

            @pl.when(turn + 1 < ROUNDS)
            def _():
                window[1, OWN, place, :] = result[place, :]

                @pl.when((lax.rem(order, 2) == 1) & (order // 2 < BATCH))
                def _():
                    own_copies(1, order // 2, start)

                @pl.when(lax.rem(order, 2) == 1)
                def _():
                    transit_copies(1, order // 2, start)

                @pl.when(order == PIECES - 1)
                def _():
                    for later in range(SHIFT):
                        transit_copies(1, HALF + later, start)

            return 0

        lax.fori_loop(0, PIECES, finish, 0)
        return 0

    lax.fori_loop(0, ROUNDS, one_round, 0)

    def drain(order, _):
        store(order).wait()
        store(HALF + order).wait()
        for turn in range(ROUNDS):
            own_copies(turn, order, finish_send)
            own_copies(turn, HALF + order, finish_send)
            for kind in (
                transit_copies,
                ring_copies,
                edge_copies,
                over_copies,
                onward_copies,
            ):
                kind(turn, order, finish_send)
        return 0

    lax.fori_loop(0, HALF, drain, 0)
    for turn in range(ROUNDS):
        for order in range(HALF, HALF + SHIFT):
            transit_copies(turn, order, finish_send)
            onward_copies(turn, order, finish_send)


def solution(mesh):
    shape = (mesh.shape["gz"], mesh.shape["xy"])

    def on_device(patches, pair_leaves, pair_count):
        leaves, points, values = patches.shape
        rows = leaves * points
        vmem = pl.BlockSpec(memory_space=pltpu.VMEM)
        anywhere = pl.BlockSpec(memory_space=pl.ANY)
        out = pl.pallas_call(
            functools.partial(kernel, shape, (leaves, points)),
            out_shape=jax.ShapeDtypeStruct((rows, values), jnp.bfloat16),
            in_specs=[pl.BlockSpec(memory_space=pltpu.SMEM), vmem, anywhere],
            out_specs=anywhere,
            scratch_shapes=[
                pltpu.VMEM((ROUNDS, 7, rows, values), jnp.bfloat16),
                pltpu.VMEM((rows, values), jnp.float32),
                pltpu.VMEM((rows, points), jnp.float32),
                pltpu.VMEM((rows, points), jnp.float32),
                pltpu.VMEM((leaves, 2 * PART * points), jnp.float32),
                pltpu.VMEM((5, leaves, rows), jnp.float32),
                pltpu.VMEM((4, leaves, 128), jnp.float32),
                pltpu.VMEM((rows, values), jnp.bfloat16),
                pltpu.SemaphoreType.DMA,
                pltpu.SemaphoreType.DMA((PIECES,)),
                pltpu.SemaphoreType.DMA((ROUNDS, 7, PIECES)),
                pltpu.SemaphoreType.DMA((ROUNDS, 7, PIECES)),
                pltpu.SemaphoreType.DMA((2,)),
                pltpu.SemaphoreType.DMA((2,)),
            ],
            compiler_params=pltpu.CompilerParams(
                collective_id=0, has_side_effects=True, vmem_limit_bytes=56 << 20
            ),
            name="denoise",
        )(pair_count, pair_leaves.T, patches.reshape(rows, values))
        return out.reshape(leaves, points, values)

    return jax.shard_map(
        on_device,
        mesh=mesh,
        in_specs=(P(("gz", "xy"), None, None), P(("gz", "xy"), None), P()),
        out_specs=P(("gz", "xy"), None, None),
        check_vma=False,
    )
```

```python
import functools
import math

import jax
import jax.numpy as jnp
from jax import lax
from jax.experimental import pallas as pl
from jax.experimental.pallas import tpu as pltpu
from jax.sharding import PartitionSpec as P

MESH = pl.DeviceIdType.MESH
ROUNDS = 2
RING = 4
PIECES = 8
BATCH = 2
SHIFT = 1
HALF = PIECES // 2
PART = 2
OWN, RIGHT, LEFT, ACROSS, SIDE_A, SIDE_B, TRANSIT = range(7)
STAY, NEXT, PREV, NEXT2, PREV2 = range(5)
FIRST_AT = (1, 2, 2, 1, 2, 1, 1, 1, 9)
FIRST = (
    ((OWN, 0), (OWN, 1)), ((RIGHT, 4), (OWN, 2)), ((OWN, 3), (OWN, 4)), ((RIGHT, 5), (OWN, 5)),
    ((OWN, 6), (OWN, 7)), ((SIDE_A, 0), (ACROSS, 0)), ((ACROSS, 4), (SIDE_A, 1)), ((ACROSS, 1), (ACROSS, 5)),
    ((RIGHT, 6), (SIDE_B, 0)), ((RIGHT, 7), (SIDE_B, 4)), ((ACROSS, 6), (SIDE_B, 1)), ((ACROSS, 2), (ACROSS, 7)),
    ((SIDE_B, 5), (ACROSS, 3)), ((RIGHT, 0), (SIDE_A, 2)), ((SIDE_A, 4), (RIGHT, 1)), ((SIDE_B, 2), (SIDE_A, 5)),
    ((RIGHT, 2), (SIDE_B, 6)), ((SIDE_A, 6), (RIGHT, 3)), ((SIDE_B, 3), (SIDE_A, 7)), ((SIDE_B, 7), (SIDE_A, 3)),
)
INNER_AT = (1, 2, 2, 1, 2, 1, 2, 2, 7)
INNER = (
    ((OWN, 0), (OWN, 1)), ((LEFT, 0), (RIGHT, 4)), ((OWN, 2), (OWN, 3)), ((LEFT, 1), (RIGHT, 5)),
    ((OWN, 4), (OWN, 5)), ((ACROSS, 0), (ACROSS, 4)), ((ACROSS, 1), (ACROSS, 5)), ((OWN, 6), (OWN, 7)),
    ((SIDE_A, 0), (LEFT, 2)), ((RIGHT, 6), (SIDE_A, 4)), ((RIGHT, 7), (LEFT, 3)), ((SIDE_A, 1), (ACROSS, 6)),
    ((ACROSS, 2), (SIDE_A, 5)), ((ACROSS, 7), (ACROSS, 3)), ((SIDE_A, 2), (RIGHT, 0)), ((LEFT, 4), (SIDE_A, 6)),
    ((RIGHT, 1), (LEFT, 5)), ((SIDE_A, 3), (RIGHT, 2)), ((LEFT, 6), (SIDE_A, 7)), ((RIGHT, 3), (LEFT, 7)),
)
LAST_AT = FIRST_AT
LAST = tuple(
    tuple(
        (LEFT if block == RIGHT else block, part if block == OWN else (part + 4) % 8)
        for block, part in unit
    )
    for unit in FIRST
)


def chosen(values, index):
    result = values[0]
    for k in range(1, len(values)):
        if values[k] is not values[0]:
            result = jnp.where(index == k, values[k], result)
    return result


def split(square):
    high = square.astype(jnp.bfloat16)
    low = (square - high.astype(jnp.float32)).astype(jnp.bfloat16)
    return high, low


def squares(block):
    wide = block.astype(jnp.float32)
    return split(wide * wide)


def contract(a, b, da, db):
    return lax.dot_general(
        a, b, (((da,), (db,)), ((), ())), preferred_element_type=jnp.float32
    )


def kernel(
    shape,
    sizes,
    count_ref,
    pairs_ref,
    patches_ref,
    out_ref,
    window,
    numer,
    denom,
    target_power,
    source_row,
    extra,
    listed,
    result,
    load_sem,
    store_sem,
    block_send,
    block_recv,
    listed_send,
    listed_recv,
):
    outer, inner = shape
    leaves, points = sizes
    devices = outer * inner
    rows = leaves * points
    chunk = rows // PIECES
    width = PART * points
    parts_here = leaves // PART
    per_part = PIECES // parts_here
    spread = patches_ref.shape[1] / 4.0
    scale = math.log2(math.e) / spread
    me = lax.axis_index("gz") * inner + lax.axis_index("xy")
    row, z = me // RING, lax.rem(me, RING)

    def device(step):
        index = lax.rem(me + step + devices, devices)
        return (index // inner, lax.rem(index, inner))

    def along(step):
        index = row * RING + lax.rem(z + step + RING, RING)
        return (index // inner, lax.rem(index, inner))

    right, left = along(1), along(-1)
    up, down = device(RING), device(-RING)
    first, last = z == 0, z == RING - 1
    edge = first | last
    toward = lax.rem(me + jnp.where(z < 2, RING, -RING) + devices, devices)
    over = (toward // inner, lax.rem(toward, inner))

    load = pltpu.make_async_copy(patches_ref, window.at[0, OWN], load_sem)
    load.start()

    barrier = pltpu.get_barrier_semaphore()
    peers = (right, left, up, down, device(1), device(-1), device(2), device(-2))
    for peer in peers:
        pl.semaphore_signal(barrier, inc=1, device_id=peer, device_id_type=MESH)

    def moved(turn, flow, source, slot, piece, target):
        place = pl.ds(pl.multiple_of(piece * chunk, chunk), chunk)
        return pltpu.make_async_remote_copy(
            src_ref=window.at[turn, source, place],
            dst_ref=window.at[turn, slot, place],
            send_sem=block_send.at[turn, flow, piece],
            recv_sem=block_recv.at[turn, slot, piece],
            device_id=target,
            device_id_type=MESH,
        )

    def arrived(turn, slot, piece):
        moved(turn, 0, OWN, slot, piece, right).wait_recv()

    def start(copy):
        copy.start()

    def finish_send(copy):
        copy.wait_send()

    def own_copies(turn, order, act):
        @pl.when((order < HALF) | jnp.logical_not(last))
        def _():
            act(moved(turn, 0, OWN, LEFT, order, right))

        @pl.when((order < HALF) | jnp.logical_not(first))
        def _():
            act(moved(turn, 1, OWN, RIGHT, lax.rem(order + HALF, PIECES), left))

    def passing(order):
        at_last = jnp.where(order < HALF, HALF + order, order - SHIFT)
        return lax.rem(at_last + HALF, PIECES), at_last

    def transit_copies(turn, order, act):
        at_first, at_last = passing(order)

        @pl.when(first)
        def _():
            act(moved(turn, 2, OWN, TRANSIT, at_first, down))

        @pl.when(last)
        def _():
            act(moved(turn, 2, OWN, TRANSIT, at_last, up))

    def ring_copies(turn, order, act):
        act(moved(turn, 3, LEFT, ACROSS, order, right))
        act(moved(turn, 3, RIGHT, ACROSS, HALF + order, left))

    def edge_copies(turn, order, act):
        @pl.when(first & (order < HALF - SHIFT))
        def _():
            act(moved(turn, 4, LEFT, SIDE_A, order, up))

        @pl.when(last & (order < HALF - SHIFT))
        def _():
            act(moved(turn, 4, RIGHT, SIDE_A, HALF + order, down))

    def over_copies(turn, order, act):
        for piece in (order, HALF + order):

            @pl.when(edge)
            def _():
                act(moved(turn, 5, ACROSS, SIDE_B, piece, over))

            @pl.when(jnp.logical_not(edge))
            def _():
                act(moved(turn, 5, ACROSS, SIDE_A, piece, over))

    def onward_copies(turn, order, act):
        at_first, at_last = passing(order)

        @pl.when(first)
        def _():
            act(moved(turn, 6, TRANSIT, SIDE_A, at_first, left))

        @pl.when(last)
        def _():
            act(moved(turn, 6, TRANSIT, SIDE_A, at_last, right))

    def pass_on(turn, order):
        at_first, at_last = passing(order)

        @pl.when(first)
        def _():
            arrived(turn, TRANSIT, at_first)

        @pl.when(last)
        def _():
            arrived(turn, TRANSIT, at_last)

        onward_copies(turn, order, start)

    def send_rest(turn, order):
        own_copies(turn, order, start)

        @pl.when(order >= HALF)
        def _():
            pass_on(turn, order - HALF)

    def transfers(turn, at):
        batch, place = (at - 1) // (2 * BATCH), lax.rem(at - 1, 2 * BATCH)
        order = BATCH * batch + lax.rem(place, BATCH)

        @pl.when((at > 0) & (place < BATCH))
        def _():
            arrived(turn, LEFT, order)
            arrived(turn, RIGHT, HALF + order)
            ring_copies(turn, order, start)
            edge_copies(turn, order, start)

        @pl.when((at > 0) & (place >= BATCH))
        def _():
            send_rest(turn, order + BATCH)
            arrived(turn, ACROSS, order)
            arrived(turn, ACROSS, HALF + order)
            over_copies(turn, order, start)

        @pl.when(at == PIECES)
        def _():
            for later in range(BATCH, HALF):
                send_rest(turn, HALF + later)
            for later in range(SHIFT):
                pass_on(turn, HALF + later)

    pl.semaphore_wait(barrier, len(peers))
    load.wait()
    for order in range(BATCH):
        own_copies(0, order, start)

    def send_transit(order, _):
        transit_copies(0, order, start)
        return 0

    lax.fori_loop(0, HALF + SHIFT, send_transit, 0)

    slots = pairs_ref.shape[1]
    lanes = 128
    leaf = lax.broadcasted_iota(jnp.int32, (lanes, slots), 0) + me * leaves
    live = lax.broadcasted_iota(jnp.int32, (lanes, slots), 1) < count_ref[me]
    one_a = jnp.where(live & (pairs_ref[0:1, :] == leaf), 1.0, 0.0).astype(jnp.bfloat16)
    one_b = jnp.where(live & (pairs_ref[1:2, :] == leaf), 1.0, 0.0).astype(jnp.bfloat16)
    forward = contract(one_a, one_b, 1, 1)
    backward = contract(one_b, one_a, 1, 1)
    listed[0] = backward[leaves : 2 * leaves]
    listed[1] = backward[2 * leaves : 3 * leaves]

    def listed_copy(k):
        return pltpu.make_async_remote_copy(
            src_ref=listed.at[k],
            dst_ref=listed.at[2 + k],
            send_sem=listed_send.at[k],
            recv_sem=listed_recv.at[k],
            device_id=device(k + 1),
            device_id_type=MESH,
        )

    for k in range(2):
        listed_copy(k).start()

    def store(piece):
        place = pl.ds(pl.multiple_of(piece * chunk, chunk), chunk)
        return pltpu.make_async_copy(result.at[place], out_ref.at[place], store_sem.at[piece])

    def begin_round(turn):
        high, low = squares(window[turn, OWN])
        ones = jnp.ones((high.shape[1], points), jnp.bfloat16)
        target_power[...] = scale * (contract(high, ones, 1, 0) + contract(low, ones, 1, 0))
        numer[...] = jnp.zeros_like(numer)
        denom[...] = jnp.zeros_like(denom)

    def tabulate(counts, steps):
        counts = jnp.concatenate(counts, axis=0).astype(jnp.bfloat16)
        place = lax.broadcasted_iota(jnp.int32, (lanes, rows), 0)
        at = lax.broadcasted_iota(jnp.int32, (lanes, rows), 1) - place * points
        spots = jnp.where((at >= 0) & (at < points), 1.0, 0.0).astype(jnp.bfloat16)
        wide = contract(counts, spots, 1, 0)
        wide = jnp.where(wide > 0.0, jnp.log2(wide), -jnp.inf)
        for k, step in enumerate(steps):
            extra[step] = wide[k * leaves : (k + 1) * leaves]

    begin_round(0)
    ahead = forward[:leaves]
    tabulate(
        [
            ahead + backward[:leaves],
            pltpu.roll(ahead, lanes - leaves, 1),
            pltpu.roll(ahead, lanes - 2 * leaves, 1),
        ],
        (STAY, NEXT, NEXT2),
    )

    def unit(turn, number):
        sources, rows_here = [], []
        for half in range(2):
            codes = [
                jnp.where(
                    first,
                    8 * f[half][0] + f[half][1],
                    jnp.where(last, 8 * l[half][0] + l[half][1], 8 * i[half][0] + i[half][1]),
                )
                for f, i, l in zip(FIRST, INNER, LAST)
            ]
            code = chosen(codes, number)
            slot, part = code // 8, lax.rem(code, 8)
            side = (slot == SIDE_A) | (slot == SIDE_B)
            late = ((slot == LEFT) & (part >= 4)) | ((slot == RIGHT) & (part < 4))

            @pl.when(side | late)
            def _():
                for k in range(per_part):
                    arrived(turn, slot, part * per_part + k)

            near = jnp.where(first, PREV, jnp.where(z == 1, PREV2, jnp.where(last, NEXT, NEXT2)))
            far = jnp.where(z < 2, NEXT2, PREV2)
            beyond = jnp.where(first, PREV2, NEXT2)
            step = chosen((STAY, NEXT, PREV, far, near, beyond), slot)
            place = pl.ds(pl.multiple_of(part * width, width), width)
            sources.append(window[turn, slot, place, :])
            rows_here.append(extra[step, :, place])
        source = jnp.concatenate(sources, axis=0)
        wide = source.astype(jnp.float32)
        wide = wide * wide
        folded = wide[:, :points] + wide[:, points:]
        power = [
            jnp.sum(folded[s * points : (s + 1) * points].T, axis=0, keepdims=True)
            for s in range(2 * PART)
        ]
        source_row[...] = jnp.concatenate(power, axis=1) * scale - jnp.concatenate(
            rows_here, axis=1
        )
        cross = contract(window[turn, OWN], source, 1, 1)
        parts = []
        for t in range(leaves):
            span = slice(t * points, (t + 1) * points)
            total, part = None, []
            for s in range(2 * PART):
                lanes_here = slice(s * points, (s + 1) * points)
                away = target_power[span, :] + source_row[t : t + 1, lanes_here]
                weight = jnp.exp2(cross[span, lanes_here] * (2.0 * scale) - away)
                total = weight if total is None else total + weight
                part.append(weight.astype(jnp.bfloat16))
            denom[span, :] += total
            parts.append(jnp.concatenate(part, axis=1))
        weights = jnp.concatenate(parts, axis=0)
        numer[...] += jnp.dot(weights, source, preferred_element_type=jnp.float32)

    def one_round(turn, _):
        @pl.when(turn > 0)
        def _():
            begin_round(turn)

        def step(at, done):
            transfers(turn, at)

            @pl.when((turn == 0) & (at == 1))
            def _():
                for k in range(2):
                    listed_copy(k).wait()
                tabulate([listed[2], listed[3]], (PREV, PREV2))

            more = chosen(
                [
                    jnp.where(first | last, e, i) if e != i else e
                    for e, i in zip(FIRST_AT, INNER_AT)
                ],
                at,
            )

            def each(k, _):
                unit(turn, done + k)
                return 0

            lax.fori_loop(0, more, each, 0)
            return done + more

        lax.fori_loop(0, len(FIRST_AT), step, 0)

        def finish(order, _):
            for piece in (order, HALF + order):
                place = pl.ds(pl.multiple_of(piece * chunk, chunk), chunk)
                below = 1.0 + jnp.sum(denom[place, :], axis=1, keepdims=True)
                above = window[turn, OWN, place, :].astype(jnp.float32) + numer[place, :]
                result[place, :] = (above * (1.0 / below)).astype(jnp.bfloat16)

            @pl.when(turn + 1 == ROUNDS)
            def _():
                store(order).start()
                store(HALF + order).start()

            @pl.when(turn + 1 < ROUNDS)
            def _():
                for piece in (order, HALF + order):
                    place = pl.ds(pl.multiple_of(piece * chunk, chunk), chunk)
                    window[1, OWN, place, :] = result[place, :]

                @pl.when(order < BATCH)
                def _():
                    own_copies(1, order, start)

                transit_copies(1, order, start)

                @pl.when(order == HALF - 1)
                def _():
                    for later in range(SHIFT):
                        transit_copies(1, HALF + later, start)

            return 0

        lax.fori_loop(0, HALF, finish, 0)
        return 0

    lax.fori_loop(0, ROUNDS, one_round, 0)

    def drain(order, _):
        store(order).wait()
        store(HALF + order).wait()
        for turn in range(ROUNDS):
            own_copies(turn, order, finish_send)
            own_copies(turn, HALF + order, finish_send)
            for kind in (
                transit_copies,
                ring_copies,
                edge_copies,
                over_copies,
                onward_copies,
            ):
                kind(turn, order, finish_send)
        return 0

    lax.fori_loop(0, HALF, drain, 0)
    for turn in range(ROUNDS):
        for order in range(HALF, HALF + SHIFT):
            transit_copies(turn, order, finish_send)
            onward_copies(turn, order, finish_send)


def solution(mesh):
    shape = (mesh.shape["gz"], mesh.shape["xy"])

    def on_device(patches, pair_leaves, pair_count):
        leaves, points, values = patches.shape
        rows = leaves * points
        vmem = pl.BlockSpec(memory_space=pltpu.VMEM)
        anywhere = pl.BlockSpec(memory_space=pl.ANY)
        out = pl.pallas_call(
            functools.partial(kernel, shape, (leaves, points)),
            out_shape=jax.ShapeDtypeStruct((rows, values), jnp.bfloat16),
            in_specs=[pl.BlockSpec(memory_space=pltpu.SMEM), vmem, anywhere],
            out_specs=anywhere,
            scratch_shapes=[
                pltpu.VMEM((ROUNDS, 7, rows, values), jnp.bfloat16),
                pltpu.VMEM((rows, values), jnp.float32),
                pltpu.VMEM((rows, points), jnp.float32),
                pltpu.VMEM((rows, points), jnp.float32),
                pltpu.VMEM((leaves, 2 * PART * points), jnp.float32),
                pltpu.VMEM((5, leaves, rows), jnp.float32),
                pltpu.VMEM((4, leaves, 128), jnp.float32),
                pltpu.VMEM((rows, values), jnp.bfloat16),
                pltpu.SemaphoreType.DMA,
                pltpu.SemaphoreType.DMA((PIECES,)),
                pltpu.SemaphoreType.DMA((ROUNDS, 7, PIECES)),
                pltpu.SemaphoreType.DMA((ROUNDS, 7, PIECES)),
                pltpu.SemaphoreType.DMA((2,)),
                pltpu.SemaphoreType.DMA((2,)),
            ],
            compiler_params=pltpu.CompilerParams(
                collective_id=0, has_side_effects=True, vmem_limit_bytes=56 << 20
            ),
            name="denoise",
        )(pair_count, pair_leaves.T, patches.reshape(rows, values))
        return out.reshape(leaves, points, values)

    return jax.shard_map(
        on_device,
        mesh=mesh,
        in_specs=(P(("gz", "xy"), None, None), P(("gz", "xy"), None), P()),
        out_specs=P(("gz", "xy"), None, None),
        check_vma=False,
    )
```

```python
import functools
import math

import jax
import jax.numpy as jnp
from jax import lax
from jax.experimental import pallas as pl
from jax.experimental.pallas import tpu as pltpu
from jax.sharding import PartitionSpec as P

MESH = pl.DeviceIdType.MESH
ROUNDS = 2
RING = 4
PIECES = 8
BATCH = 2
SHIFT = 1
HALF = PIECES // 2
PART = 2
OWN, RIGHT, LEFT, ACROSS, SIDE_A, SIDE_B, TRANSIT = range(7)
STAY, NEXT, PREV, NEXT2, PREV2 = range(5)
FIRST_AT = (1, 2, 2, 1, 2, 1, 1, 1, 9)
FIRST = (
    ((OWN, 0), (OWN, 1)), ((RIGHT, 4), (OWN, 2)), ((OWN, 3), (OWN, 4)), ((RIGHT, 5), (OWN, 5)),
    ((OWN, 6), (OWN, 7)), ((SIDE_A, 0), (ACROSS, 0)), ((ACROSS, 4), (SIDE_A, 1)), ((ACROSS, 1), (ACROSS, 5)),
    ((RIGHT, 6), (SIDE_B, 0)), ((RIGHT, 7), (SIDE_B, 4)), ((ACROSS, 6), (SIDE_B, 1)), ((ACROSS, 2), (ACROSS, 7)),
    ((SIDE_B, 5), (ACROSS, 3)), ((RIGHT, 0), (SIDE_A, 2)), ((SIDE_A, 4), (RIGHT, 1)), ((SIDE_B, 2), (SIDE_A, 5)),
    ((RIGHT, 2), (SIDE_B, 6)), ((SIDE_A, 6), (RIGHT, 3)), ((SIDE_B, 3), (SIDE_A, 7)), ((SIDE_B, 7), (SIDE_A, 3)),
)
INNER_AT = (1, 2, 2, 1, 2, 1, 2, 2, 7)
INNER = (
    ((OWN, 0), (OWN, 1)), ((LEFT, 0), (RIGHT, 4)), ((OWN, 2), (OWN, 3)), ((LEFT, 1), (RIGHT, 5)),
    ((OWN, 4), (OWN, 5)), ((ACROSS, 0), (ACROSS, 4)), ((ACROSS, 1), (ACROSS, 5)), ((OWN, 6), (OWN, 7)),
    ((SIDE_A, 0), (LEFT, 2)), ((RIGHT, 6), (SIDE_A, 4)), ((RIGHT, 7), (LEFT, 3)), ((SIDE_A, 1), (ACROSS, 6)),
    ((ACROSS, 2), (SIDE_A, 5)), ((ACROSS, 7), (ACROSS, 3)), ((SIDE_A, 2), (RIGHT, 0)), ((LEFT, 4), (SIDE_A, 6)),
    ((RIGHT, 1), (LEFT, 5)), ((SIDE_A, 3), (RIGHT, 2)), ((LEFT, 6), (SIDE_A, 7)), ((RIGHT, 3), (LEFT, 7)),
)
LAST_AT = FIRST_AT
LAST = tuple(
    tuple(
        (LEFT if block == RIGHT else block, part if block == OWN else (part + 4) % 8)
        for block, part in unit
    )
    for unit in FIRST
)


def chosen(values, index):
    result = values[0]
    for k in range(1, len(values)):
        if values[k] is not values[0]:
            result = jnp.where(index == k, values[k], result)
    return result


def split(square):
    high = square.astype(jnp.bfloat16)
    low = (square - high.astype(jnp.float32)).astype(jnp.bfloat16)
    return high, low


def squares(block):
    wide = block.astype(jnp.float32)
    return split(wide * wide)


def contract(a, b, da, db):
    return lax.dot_general(
        a, b, (((da,), (db,)), ((), ())), preferred_element_type=jnp.float32
    )


def kernel(
    shape,
    sizes,
    count_ref,
    pairs_ref,
    patches_ref,
    out_ref,
    window,
    numer,
    denom,
    target_power,
    source_row,
    extra,
    listed,
    result,
    load_sem,
    store_sem,
    block_send,
    block_recv,
    listed_send,
    listed_recv,
):
    outer, inner = shape
    leaves, points = sizes
    devices = outer * inner
    rows = leaves * points
    chunk = rows // PIECES
    width = PART * points
    parts_here = leaves // PART
    per_part = PIECES // parts_here
    spread = patches_ref.shape[1] / 4.0
    scale = math.log2(math.e) / spread
    me = lax.axis_index("gz") * inner + lax.axis_index("xy")
    row, z = me // RING, lax.rem(me, RING)

    def device(step):
        index = lax.rem(me + step + devices, devices)
        return (index // inner, lax.rem(index, inner))

    def along(step):
        index = row * RING + lax.rem(z + step + RING, RING)
        return (index // inner, lax.rem(index, inner))

    right, left = along(1), along(-1)
    up, down = device(RING), device(-RING)
    first, last = z == 0, z == RING - 1
    edge = first | last
    toward = lax.rem(me + jnp.where(z < 2, RING, -RING) + devices, devices)
    over = (toward // inner, lax.rem(toward, inner))

    load = pltpu.make_async_copy(patches_ref, window.at[0, OWN], load_sem)
    load.start()

    barrier = pltpu.get_barrier_semaphore()
    peers = (right, left, up, down, device(1), device(-1), device(2), device(-2))
    for peer in peers:
        pl.semaphore_signal(barrier, inc=1, device_id=peer, device_id_type=MESH)

    def moved(turn, flow, source, slot, piece, target):
        place = pl.ds(pl.multiple_of(piece * chunk, chunk), chunk)
        return pltpu.make_async_remote_copy(
            src_ref=window.at[turn, source, place],
            dst_ref=window.at[turn, slot, place],
            send_sem=block_send.at[turn, flow, piece],
            recv_sem=block_recv.at[turn, slot, piece],
            device_id=target,
            device_id_type=MESH,
        )

    def arrived(turn, slot, piece):
        moved(turn, 0, OWN, slot, piece, right).wait_recv()

    def start(copy):
        copy.start()

    def finish_send(copy):
        copy.wait_send()

    def own_copies(turn, order, act):
        @pl.when((order < HALF) | jnp.logical_not(last))
        def _():
            act(moved(turn, 0, OWN, LEFT, order, right))

        @pl.when((order < HALF) | jnp.logical_not(first))
        def _():
            act(moved(turn, 1, OWN, RIGHT, lax.rem(order + HALF, PIECES), left))

    def passing(order):
        at_last = jnp.where(order < HALF, HALF + order, order - SHIFT)
        return lax.rem(at_last + HALF, PIECES), at_last

    def transit_copies(turn, order, act):
        at_first, at_last = passing(order)

        @pl.when(first)
        def _():
            act(moved(turn, 2, OWN, TRANSIT, at_first, down))

        @pl.when(last)
        def _():
            act(moved(turn, 2, OWN, TRANSIT, at_last, up))

    def ring_copies(turn, order, act):
        act(moved(turn, 3, LEFT, ACROSS, order, right))
        act(moved(turn, 3, RIGHT, ACROSS, HALF + order, left))

    def edge_copies(turn, order, act):
        @pl.when(first & (order < HALF - SHIFT))
        def _():
            act(moved(turn, 4, LEFT, SIDE_A, order, up))

        @pl.when(last & (order < HALF - SHIFT))
        def _():
            act(moved(turn, 4, RIGHT, SIDE_A, HALF + order, down))

    def over_copy(turn, piece):
        return moved(turn, 5, ACROSS, jnp.where(edge, SIDE_B, SIDE_A), piece, over)

    def over_copies(turn, order, act):
        for piece in (order, HALF + order):
            act(over_copy(turn, piece))

    def onward_copies(turn, order, act):
        at_first, at_last = passing(order)

        @pl.when(first)
        def _():
            act(moved(turn, 6, TRANSIT, SIDE_A, at_first, left))

        @pl.when(last)
        def _():
            act(moved(turn, 6, TRANSIT, SIDE_A, at_last, right))

    def pass_on(turn, order):
        at_first, at_last = passing(order)

        @pl.when(first)
        def _():
            arrived(turn, TRANSIT, at_first)

        @pl.when(last)
        def _():
            arrived(turn, TRANSIT, at_last)

        onward_copies(turn, order, start)

    def send_rest(turn, order):
        own_copies(turn, order, start)

        @pl.when(order >= HALF)
        def _():
            pass_on(turn, order - HALF)

    def transfers(turn, at):
        batch, place = (at - 1) // (2 * BATCH), lax.rem(at - 1, 2 * BATCH)
        order = BATCH * batch + lax.rem(place, BATCH)

        @pl.when((at > 0) & (place < BATCH))
        def _():
            arrived(turn, LEFT, order)
            arrived(turn, RIGHT, HALF + order)
            ring_copies(turn, order, start)
            edge_copies(turn, order, start)

        @pl.when((at > 0) & (place >= BATCH))
        def _():
            send_rest(turn, order + BATCH)
            for piece in (order, HALF + order):
                arrived(turn, ACROSS, piece)
                over_copy(turn, piece).start()

        @pl.when(at == PIECES)
        def _():
            for later in range(BATCH, HALF):
                send_rest(turn, HALF + later)
            for later in range(SHIFT):
                pass_on(turn, HALF + later)

    pl.semaphore_wait(barrier, len(peers))
    load.wait()
    for order in range(BATCH):
        own_copies(0, order, start)

    def send_transit(order, _):
        transit_copies(0, order, start)
        return 0

    lax.fori_loop(0, HALF + SHIFT, send_transit, 0)

    slots = pairs_ref.shape[1]
    lanes = 128
    leaf = lax.broadcasted_iota(jnp.int32, (lanes, slots), 0) + me * leaves
    live = lax.broadcasted_iota(jnp.int32, (lanes, slots), 1) < count_ref[me]
    one_a = jnp.where(live & (pairs_ref[0:1, :] == leaf), 1.0, 0.0).astype(jnp.bfloat16)
    one_b = jnp.where(live & (pairs_ref[1:2, :] == leaf), 1.0, 0.0).astype(jnp.bfloat16)
    forward = contract(one_a, one_b, 1, 1)
    backward = contract(one_b, one_a, 1, 1)
    listed[0] = backward[leaves : 2 * leaves]
    listed[1] = backward[2 * leaves : 3 * leaves]

    def listed_copy(k):
        return pltpu.make_async_remote_copy(
            src_ref=listed.at[k],
            dst_ref=listed.at[2 + k],
            send_sem=listed_send.at[k],
            recv_sem=listed_recv.at[k],
            device_id=device(k + 1),
            device_id_type=MESH,
        )

    for k in range(2):
        listed_copy(k).start()

    def store(piece):
        place = pl.ds(pl.multiple_of(piece * chunk, chunk), chunk)
        return pltpu.make_async_copy(result.at[place], out_ref.at[place], store_sem.at[piece])

    def begin_round(turn):
        high, low = squares(window[turn, OWN])
        ones = jnp.ones((high.shape[1], points), jnp.bfloat16)
        target_power[...] = scale * (contract(high, ones, 1, 0) + contract(low, ones, 1, 0))
        numer[...] = jnp.zeros_like(numer)
        denom[...] = jnp.zeros_like(denom)

    def tabulate(counts, steps):
        counts = jnp.concatenate(counts, axis=0).astype(jnp.bfloat16)
        place = lax.broadcasted_iota(jnp.int32, (lanes, rows), 0)
        at = lax.broadcasted_iota(jnp.int32, (lanes, rows), 1) - place * points
        spots = jnp.where((at >= 0) & (at < points), 1.0, 0.0).astype(jnp.bfloat16)
        wide = contract(counts, spots, 1, 0)
        wide = jnp.where(wide > 0.0, jnp.log2(wide), -jnp.inf)
        for k, step in enumerate(steps):
            extra[step] = wide[k * leaves : (k + 1) * leaves]

    begin_round(0)
    ahead = forward[:leaves]
    tabulate(
        [
            ahead + backward[:leaves],
            pltpu.roll(ahead, lanes - leaves, 1),
            pltpu.roll(ahead, lanes - 2 * leaves, 1),
        ],
        (STAY, NEXT, NEXT2),
    )

    def unit(turn, number):
        sources, rows_here = [], []
        for half in range(2):
            codes = [
                jnp.where(
                    first,
                    8 * f[half][0] + f[half][1],
                    jnp.where(last, 8 * l[half][0] + l[half][1], 8 * i[half][0] + i[half][1]),
                )
                for f, i, l in zip(FIRST, INNER, LAST)
            ]
            code = chosen(codes, number)
            slot, part = code // 8, lax.rem(code, 8)
            side = (slot == SIDE_A) | (slot == SIDE_B)
            late = ((slot == LEFT) & (part >= 4)) | ((slot == RIGHT) & (part < 4))

            @pl.when(side | late)
            def _():
                for k in range(per_part):
                    arrived(turn, slot, part * per_part + k)

            near = jnp.where(first, PREV, jnp.where(z == 1, PREV2, jnp.where(last, NEXT, NEXT2)))
            far = jnp.where(z < 2, NEXT2, PREV2)
            beyond = jnp.where(first, PREV2, NEXT2)
            step = chosen((STAY, NEXT, PREV, far, near, beyond), slot)
            place = pl.ds(pl.multiple_of(part * width, width), width)
            sources.append(window[turn, slot, place, :])
            rows_here.append(extra[step, :, place])
        source = jnp.concatenate(sources, axis=0)
        wide = source.astype(jnp.float32)
        wide = wide * wide
        folded = wide[:, :points] + wide[:, points:]
        power = [
            jnp.sum(folded[s * points : (s + 1) * points].T, axis=0, keepdims=True)
            for s in range(2 * PART)
        ]
        source_row[...] = jnp.concatenate(power, axis=1) * scale - jnp.concatenate(
            rows_here, axis=1
        )
        cross = contract(window[turn, OWN], source, 1, 1)
        parts = []
        for t in range(leaves):
            span = slice(t * points, (t + 1) * points)
            total, part = None, []
            for s in range(2 * PART):
                lanes_here = slice(s * points, (s + 1) * points)
                away = target_power[span, :] + source_row[t : t + 1, lanes_here]
                weight = jnp.exp2(cross[span, lanes_here] * (2.0 * scale) - away)
                total = weight if total is None else total + weight
                part.append(weight.astype(jnp.bfloat16))
            denom[span, :] += total
            parts.append(jnp.concatenate(part, axis=1))
        weights = jnp.concatenate(parts, axis=0)
        numer[...] += jnp.dot(weights, source, preferred_element_type=jnp.float32)

    def one_round(turn, _):
        @pl.when(turn > 0)
        def _():
            begin_round(turn)

        def step(at, done):
            transfers(turn, at)

            @pl.when((turn == 0) & (at == 1))
            def _():
                for k in range(2):
                    listed_copy(k).wait()
                tabulate([listed[2], listed[3]], (PREV, PREV2))

            more = chosen(
                [
                    jnp.where(first | last, e, i) if e != i else e
                    for e, i in zip(FIRST_AT, INNER_AT)
                ],
                at,
            )

            def each(k, _):
                unit(turn, done + k)
                return 0

            lax.fori_loop(0, more, each, 0)
            return done + more

        lax.fori_loop(0, len(FIRST_AT), step, 0)

        def finish(order, _):
            for piece in (order, HALF + order):
                place = pl.ds(pl.multiple_of(piece * chunk, chunk), chunk)
                below = 1.0 + jnp.sum(denom[place, :], axis=1, keepdims=True)
                above = window[turn, OWN, place, :].astype(jnp.float32) + numer[place, :]
                result[place, :] = (above * (1.0 / below)).astype(jnp.bfloat16)

            @pl.when(turn + 1 == ROUNDS)
            def _():
                store(order).start()
                store(HALF + order).start()

            @pl.when(turn + 1 < ROUNDS)
            def _():
                for piece in (order, HALF + order):
                    place = pl.ds(pl.multiple_of(piece * chunk, chunk), chunk)
                    window[1, OWN, place, :] = result[place, :]

                @pl.when(order < BATCH)
                def _():
                    own_copies(1, order, start)

                transit_copies(1, order, start)

                @pl.when(order == HALF - 1)
                def _():
                    for later in range(SHIFT):
                        transit_copies(1, HALF + later, start)

            return 0

        lax.fori_loop(0, HALF, finish, 0)
        return 0

    lax.fori_loop(0, ROUNDS, one_round, 0)

    def drain(order, _):
        store(order).wait()
        store(HALF + order).wait()
        for turn in range(ROUNDS):
            own_copies(turn, order, finish_send)
            own_copies(turn, HALF + order, finish_send)
            for kind in (
                transit_copies,
                ring_copies,
                edge_copies,
                over_copies,
                onward_copies,
            ):
                kind(turn, order, finish_send)
        return 0

    lax.fori_loop(0, HALF, drain, 0)
    for turn in range(ROUNDS):
        for order in range(HALF, HALF + SHIFT):
            transit_copies(turn, order, finish_send)
            onward_copies(turn, order, finish_send)


def solution(mesh):
    shape = (mesh.shape["gz"], mesh.shape["xy"])

    def on_device(patches, pair_leaves, pair_count):
        leaves, points, values = patches.shape
        rows = leaves * points
        vmem = pl.BlockSpec(memory_space=pltpu.VMEM)
        anywhere = pl.BlockSpec(memory_space=pl.ANY)
        out = pl.pallas_call(
            functools.partial(kernel, shape, (leaves, points)),
            out_shape=jax.ShapeDtypeStruct((rows, values), jnp.bfloat16),
            in_specs=[pl.BlockSpec(memory_space=pltpu.SMEM), vmem, anywhere],
            out_specs=anywhere,
            scratch_shapes=[
                pltpu.VMEM((ROUNDS, 7, rows, values), jnp.bfloat16),
                pltpu.VMEM((rows, values), jnp.float32),
                pltpu.VMEM((rows, points), jnp.float32),
                pltpu.VMEM((rows, points), jnp.float32),
                pltpu.VMEM((leaves, 2 * PART * points), jnp.float32),
                pltpu.VMEM((5, leaves, rows), jnp.float32),
                pltpu.VMEM((4, leaves, 128), jnp.float32),
                pltpu.VMEM((rows, values), jnp.bfloat16),
                pltpu.SemaphoreType.DMA,
                pltpu.SemaphoreType.DMA((PIECES,)),
                pltpu.SemaphoreType.DMA((ROUNDS, 7, PIECES)),
                pltpu.SemaphoreType.DMA((ROUNDS, 7, PIECES)),
                pltpu.SemaphoreType.DMA((2,)),
                pltpu.SemaphoreType.DMA((2,)),
            ],
            compiler_params=pltpu.CompilerParams(
                collective_id=0, has_side_effects=True, vmem_limit_bytes=56 << 20
            ),
            name="denoise",
        )(pair_count, pair_leaves.T, patches.reshape(rows, values))
        return out.reshape(leaves, points, values)

    return jax.shard_map(
        on_device,
        mesh=mesh,
        in_specs=(P(("gz", "xy"), None, None), P(("gz", "xy"), None), P()),
        out_specs=P(("gz", "xy"), None, None),
        check_vma=False,
    )
```
